128 devices in a mesh: row: 8 (over y, core), col: 16 (over x, z).
Axes of the slice: x: 4, y: 4, z: 4, core: 2. Of those that a mesh axis runs over, the one named last changes fastest.
Arguments:
- blocks: bfloat16 [256, 16, 512, 512], P('row', 'col'), may hold values from 3.8146973e-06 to 0.32348633, as said below
- source_ids: int32 [256, 16], P('row', 'col'), may hold values from 0 to 255, as said below
- emission: bfloat16 [5008, 131072], P('col', 'row'), may hold values from 0.05 to 5120, as said below
- tokens: int32 [4, 104], replicated, may hold values from 0 to 5007, as said below
Outputs:
- posterior: bfloat16 [104, 131072], P(None, ('row', 'col'))
- log_total: float32 [104], replicated
The draws below stay inside these ranges and needn't reach their ends.
Inputs may be any that keep to these rules, and one draw needn't show every extreme that they name: Block id source_ids[J, k] lies in the group g of 2 consecutive blocks (g = id // 2) with g % 16 == k // (16 // 16). In every step exactly 26 of the 104 tokens lie in one range of 5008 // 16 consecutive ids, which one is drawn, and no such range holds more. `emission`: positive weights. `blocks`: positive weights.
All inputs are finite; a program needn't handle non-finite values.
Results may differ from the reference program's by a relative error of at most 0.029.
Values may be sent and summed in bfloat16 or wider, within the bound.
A program may use at most 128 MiB of HBM per device.

```python
import math
import jax
import jax.numpy as jnp
from jax import lax

STATES = 131072
BLOCK = 512
SLOTS = 16
VOCAB = 5008
STEPS = 3
SEQS = 104
CAP = 26
NB = 256
PIECE_BLOCKS = 2
N_ROW = 8
N_COL = 16


def draw_blocks(key, part):
    key = jax.random.fold_in(key, 14)
    value_key, slot_key = jax.random.split(key)
    cutoff = 0.97
    height = 200.0
    uniform_values = jax.random.uniform(value_key, (NB, SLOTS, BLOCK, BLOCK), jnp.float32)
    peaks = jnp.maximum(uniform_values - cutoff, 0.0) * (height / (1.0 - cutoff))
    diagonal = 4.0 * BLOCK * jnp.eye(BLOCK, dtype=jnp.float32)
    slot_scale = jnp.exp(jax.random.uniform(slot_key, (NB, SLOTS, 1, 1), jnp.float32, 0.0, math.log(32.0)))
    values = 1.0 + uniform_values + peaks + diagonal[None, None, :, :]
    return (values * slot_scale / (32.0 * SLOTS * BLOCK)).astype(jnp.bfloat16)


def draw_emission(key, part):
    key = jax.random.fold_in(key, 11)
    value_key, row_key, within_key = jax.random.split(key, 3)
    position = jnp.arange(STATES, dtype=jnp.float32) / STATES
    within_pattern = jnp.exp(jax.random.uniform(within_key, (VOCAB, 1, BLOCK), jnp.float32, 0.0, math.log(10.0)))
    raw_values = jnp.exp(jax.random.uniform(value_key, (VOCAB, STATES), jnp.float32, math.log(0.05), 0.0))
    row_scale = jnp.exp(jax.random.uniform(row_key, (VOCAB, 1), jnp.float32, 0.0, math.log(10.0)))
    state_scale = jnp.power(10.0, position)
    values = (raw_values * row_scale * state_scale[None, :]).reshape(VOCAB, NB, BLOCK) * within_pattern
    return values.reshape(VOCAB, STATES).astype(jnp.bfloat16)


def draw_source_ids(key, part):
    key = jax.random.fold_in(key, 12)
    row_key, within_key = jax.random.split(key)
    slots_col = SLOTS // N_COL
    group_col = jnp.arange(SLOTS, dtype=jnp.int32) // slots_col
    row_pick = jax.random.randint(row_key, (NB, SLOTS), 0, N_ROW, dtype=jnp.int32)
    within = jax.random.randint(within_key, (NB, SLOTS), 0, PIECE_BLOCKS, dtype=jnp.int32)
    return ((row_pick * N_COL + group_col[None, :]) * PIECE_BLOCKS + within).astype(jnp.int32)


def draw_tokens(key, part):
    key = jax.random.fold_in(key, 13)
    vocab_col = VOCAB // N_COL

    def single_step(step_key):
        busy_key, order_key, inner_key = jax.random.split(step_key, 3)
        busiest = jax.random.randint(busy_key, (), 0, N_COL, dtype=jnp.int32)
        position = jnp.arange(SEQS, dtype=jnp.int32)
        offset = jnp.where(position < CAP, 0, 1 + (position - CAP) % (N_COL - 1))
        owner = jax.random.permutation(order_key, (busiest + offset) % N_COL)
        inner = jax.random.randint(inner_key, (SEQS,), 0, vocab_col, dtype=jnp.int32)
        return owner * vocab_col + inner
    return jax.vmap(single_step)(jax.random.split(key, STEPS + 1)).astype(jnp.int32)


def setup_inputs(seed: int = 0) -> dict:
    splits = jax.random.split(jax.random.key(seed), 5)
    return {
        "blocks": draw_blocks(jax.random.fold_in(splits[4], 71), 0),
        "source_ids": draw_source_ids(jax.random.fold_in(splits[4], 71), 0),
        "emission": draw_emission(jax.random.fold_in(splits[4], 71), 0),
        "tokens": draw_tokens(jax.random.fold_in(splits[4], 71), 0),
    }


def reference(blocks, source_ids, emission, tokens):
    block_count = STATES // BLOCK
    slots_col = SLOTS // N_COL

    def normalize(weighted):
        scale = jnp.sum(weighted, axis=1) / STATES
        return (weighted / scale[:, None]).astype(jnp.bfloat16), jnp.log(scale)

    def transition(states_now):
        split_states = states_now.reshape(SEQS, block_count, BLOCK)

        def block_row(record):
            block_vals, source_list = record
            sources = jnp.take(split_states, source_list, axis=1).astype(jnp.float32)
            terms = jnp.einsum("bkm,kmn->kbn", sources, block_vals.astype(jnp.float32))
            grouped = jnp.sum(terms.reshape(N_COL, slots_col, SEQS, BLOCK), axis=1)
            rounded = lax.optimization_barrier(grouped.astype(jnp.bfloat16))
            return jnp.sum(rounded.astype(jnp.float32), axis=0)

        carried = lax.map(block_row, (blocks, source_ids))
        return jnp.transpose(carried, (1, 0, 2)).reshape(SEQS, STATES)

    weighted = emission[tokens[0]].astype(jnp.float32)
    states_now, log_total = normalize(weighted)
    for position in range(1, STEPS + 1):
        weighted = emission[tokens[position]].astype(jnp.float32) * transition(states_now)
        states_now, log_part = normalize(weighted)
        log_total = log_total + log_part
    return states_now, log_total
```

```python
import functools

import jax
import jax.numpy as jnp
from jax import lax
from jax.experimental import pallas as pl
from jax.experimental.pallas import tpu as pltpu
from jax.sharding import PartitionSpec as P

MESH = pl.DeviceIdType.MESH
STATES = 131072
SEQS = 104
CAP = 26
SLOT = 32
BLOCK = 512
HALF = 256
STEPS = 3
KOFF = (2, 1, 0, 3)
F32 = jnp.float32
BF16 = jnp.bfloat16


def iota(shape, dim):
    return lax.broadcasted_iota(jnp.int32, shape, dim).astype(F32)


def kernel(
    ids_ref, tok_ref, blocks_hbm, emis_hbm, post_ref, log_ref,
    blocks_v, emis_v, sel_v, pack, land1, land2, em, states_a, states_b, part, rs, wfin, ar0, ar1, ar2,
    blk_sem, emis_sem, e_send, e_recv, ag_send, ag_recv, rs_send, rs_recv, a_send, a_recv,
):
    row = lax.axis_index("row")
    col = lax.axis_index("col")
    y, core = row // 2, row % 2
    x, z = col // 4, col % 4
    vocab = emis_v.shape[1]

    def at_plane(xd, zd):
        return (row, (xd % 4) * 4 + zd % 4)

    def along(h, first, off):
        if (h == 0) == first:
            return at_plane(x + off, z)
        return at_plane(x, z + off)

    def pq(h):
        return (x, z) if h == 0 else (z, x)

    def at_y(off):
        return (((y + off) % 4) * 2 + core, col)

    sib = (row + 1 - 2 * core, col)

    def remote(src, dst, ssem, rsem, dev):
        return pltpu.make_async_remote_copy(
            src_ref=src, dst_ref=dst, send_sem=ssem, recv_sem=rsem, device_id=dev, device_id_type=MESH
        )

    def emis_copy(chunk):
        return pltpu.make_async_copy(
            emis_hbm.at[:, pl.ds(pl.multiple_of(chunk * BLOCK, BLOCK), BLOCK)], emis_v.at[chunk], emis_sem.at[chunk]
        )

    def chunk_of(h, po, qd):
        p, _ = pq(h)
        pd = (p + po) % 4
        return (pd * 4 + qd) * 2 if h == 0 else (qd * 4 + pd) * 2 + 1

    for po in (2, 1, 3, 0):
        for h in (0, 1):
            @pl.loop(0, 4)
            def _(qd):
                emis_copy(chunk_of(h, po, qd)).start()

    def blocks_copy(i):
        return pltpu.make_async_copy(blocks_hbm.at[pl.ds(i * 8, 8)], blocks_v.at[pl.ds(i * 8, 8)], blk_sem.at[i])

    for i in range(4):
        blocks_copy(i).start()

    barrier = pltpu.get_barrier_semaphore()
    row_peers = [(lax.rem(row + i, 8), col) for i in range(1, 8)]
    col_peers = [(row, lax.rem(col + i, 16)) for i in range(1, 16)]
    for dev in row_peers + col_peers:
        pl.semaphore_signal(barrier, inc=1, device_id=dev, device_id_type=MESH)

    eye = iota((SEQS, SEQS), 0) == iota((SEQS, SEQS), 1)
    before = iota((SEQS, SEQS), 0) < iota((SEQS, SEQS), 1)

    def to_col(v):
        return jnp.sum(jnp.where(eye, v, 0.0), axis=1, keepdims=True)

    def places(t):
        tok_row = tok_ref[t : t + 1, :].astype(F32)
        owner_row = jnp.zeros_like(tok_row)
        for k in range(1, 16):
            owner_row += jnp.where(tok_row >= float(k * vocab), 1.0, 0.0)
        owner_col = to_col(owner_row)
        same = jnp.where((owner_col == owner_row) & before, 1.0, 0.0)
        pos_row = jnp.sum(same, axis=0, keepdims=True)
        return tok_row, owner_row, owner_col, pos_row

    for t in range(STEPS + 1):
        tok_row, owner_row, owner_col, pos_row = places(t)
        me = col.astype(F32)
        slot_of = jnp.where((pos_row == iota((SLOT, SEQS), 0)) & (owner_row == me), 1.0, 0.0).astype(BF16)
        id_of = jnp.where(to_col(tok_row) - me * float(vocab) == iota((SEQS, vocab), 1), 1.0, 0.0).astype(BF16)
        sel_v[t * SLOT : (t + 1) * SLOT, :] = jnp.dot(slot_of, id_of, preferred_element_type=F32).astype(BF16)

    pl.semaphore_wait(barrier, 22)

    def e1(t, h, po):
        p, _ = pq(h)
        return remote(
            pack.at[t, h, po - 1], land1.at[t, h, :, p], e_send.at[t, h, 0, po - 1], e_recv.at[t, h, 0, po - 1],
            along(h, True, po),
        )

    def e2(t, h, qo):
        _, q = pq(h)
        return remote(
            land1.at[t, h, (q + qo) % 4], land2.at[t, h, q], e_send.at[t, h, 1, qo - 1], e_recv.at[t, h, 1, qo - 1],
            along(h, False, qo),
        )

    for po in (2, 1, 3, 0):
        for h in (0, 1):
            p, _ = pq(h)

            @pl.loop(0, 4)
            def _(qd):
                chunk = chunk_of(h, po, qd)
                emis_copy(chunk).wait()
                rows = jnp.dot(sel_v[...], emis_v[chunk], preferred_element_type=F32).astype(BF16)
                for t in range(STEPS + 1):
                    piece = rows[t * SLOT : (t + 1) * SLOT]
                    if po:
                        pack[t, h, po - 1, qd] = piece
                    else:
                        land1[t, h, qd, p] = piece

            if po:
                e1(0, h, po).start()

    def e_phase1(t):
        for po in (2, 1, 3):
            for h in (0, 1):
                e1(t, h, po).start()

    def e_phase2(t):
        for h in (0, 1):
            for po in (1, 3, 2):
                e1(t, h, po).wait_recv()
            for qo in (2, 1, 3):
                e2(t, h, qo).start()

    def e_final(t, h):
        p, q = pq(h)
        land2[t, h, q] = land1[t, h, q]
        _, _, owner_col, pos_row = places(t)
        if h == 0:
            high = jnp.zeros_like(owner_col)
            for k in range(1, 4):
                high += jnp.where(owner_col >= float(4 * k), 1.0, 0.0)
            place = (owner_col - 4.0 * high) * 4.0 + high
        else:
            place = owner_col
        target = place * float(SLOT) + to_col(pos_row)
        pick = jnp.where(iota((SEQS, 16 * SLOT), 1) == target, 1.0, 0.0).astype(BF16)
        for qo in (1, 3, 2):
            e2(t, h, qo).wait_recv()
        return jnp.dot(pick, land2[t, h].reshape(16 * SLOT, BLOCK), preferred_element_type=F32)

    def states_of(t):
        return states_b if t % 2 else states_a

    def ag(t, h, j, msg, of_row, dev):
        item = states_of(t).at[of_row * 2 + h, j]
        return remote(item, item, ag_send.at[t, h, j, msg], ag_recv.at[t, h, j, msg], dev)

    def same_core(off):
        return ((y + off) % 4) * 2 + core

    def ag_start(t, h, j):
        ag(t, h, j, 1, row, at_y(1)).start()
        ag(t, h, j, 2, row, at_y(3)).start()
        ag(t, h, j, 0, row, sib).start()

    def ag_relay1(t, h, j):
        for msg, off, on in ((1, 3, 1), (2, 1, 3)):
            of = same_core(off)
            ag(t, h, j, msg, of, sib).wait_recv()
            if (msg == 1) == (h == 0):
                ag(t, h, j, 5, of, at_y(on)).start()
            ag(t, h, j, msg + 2, of, sib).start()

    def ag_relay2(t, h, j):
        of = same_core(2)
        ag(t, h, j, 5, of, sib).wait_recv()
        ag(t, h, j, 6, of, sib).start()

    def ag_end(t, h, j):
        for msg in (0, 3, 4, 6):
            ag(t, h, j, msg, row, sib).wait_recv()

    def ag_sent(t, h, j):
        for msg in range(7):
            ag(t, h, j, msg, row, sib).wait_send()

    def product(t, j, h, po, k):
        p, q = pq(h)
        pd = (p + po) % 4
        qd = (q + 2 - k + 4) % 4
        dest = (pd * 4 + qd) * 2 if h == 0 else (qd * 4 + pd) * 2 + 1
        sid = ids_ref[dest]
        local = (sid // 32) * 2 + sid % 2
        left = states_of(t - 1)[local, 0]
        right = states_of(t - 1)[local, 1]
        cols = slice(j * HALF, (j + 1) * HALF)
        acc = jnp.dot(left, blocks_v[dest, :HALF, cols], preferred_element_type=F32)
        acc += jnp.dot(right, blocks_v[dest, HALF:, cols], preferred_element_type=F32)
        part[j, h, po, k] = acc.astype(BF16)

    def rcopy(t, j, h, src, msg, dev):
        return remote(src, rs.at[t % 2, j, h, msg], rs_send.at[t, j, h, msg], rs_recv.at[t, j, h, msg], dev)

    def arrived(t, j, h, msg):
        rcopy(t, j, h, rs.at[t % 2, j, h, msg], msg, sib).wait_recv()
        return rs[t % 2, j, h, msg].astype(F32)

    def rs_first(t, j):
        @pl.loop(0, 4)
        def _(k):
            for h in (0, 1):
                product(t, j, h, 2, k)
                rcopy(t, j, h, part.at[j, h, 2, k], k, along(h, True, 1 + 2 * (k % 2))).start()

        @pl.loop(0, 4)
        def _(k):
            for h in (0, 1):
                po = 3 - 2 * (k % 2)
                product(t, j, h, po, k)

    def rs_direct(t, j):
        @pl.loop(0, 4)
        def _(k):
            for h in (0, 1):
                po = 3 - 2 * (k % 2)
                rcopy(t, j, h, part.at[j, h, po, k], 8 - 4 * (k % 2) + k, along(h, True, po)).start()

    def rs_rest(t, j):
        @pl.loop(0, 4)
        def _(k):
            for h in (0, 1):
                product(t, j, h, 1 + 2 * (k % 2), k)
                product(t, j, h, 0, k)

    def rs_merge(t, j):
        @pl.loop(0, 4)
        def _(k):
            for h in (0, 1):
                po = 1 + 2 * (k % 2)
                got = arrived(t, j, h, k)
                part[j, h, po, k] = (part[j, h, po, k].astype(F32) + got).astype(BF16)
                rcopy(t, j, h, part.at[j, h, po, k], 4 + 4 * (k % 2) + k, along(h, True, po)).start()

    def summed(t, j, h, k):
        return part[j, h, 0, k].astype(F32) + arrived(t, j, h, 4 + k) + arrived(t, j, h, 8 + k)

    def rs_second(t, j):
        for k in (0, 1, 3):
            for h in (0, 1):
                part[j, h, 0, k] = summed(t, j, h, k).astype(BF16)
                src = part.at[j, h, 0, k]
                if k == 0:
                    rcopy(t, j, h, src, 12, along(h, False, 1 + 2 * j)).start()
                elif k == 1 and j == 1:
                    rcopy(t, j, h, src, 13, along(h, False, 1)).start()
                elif k == 3 and j == 0:
                    rcopy(t, j, h, src, 14, along(h, False, 3)).start()

    def rs_merge2(t, j):
        k = 1 if j == 0 else 3
        for h in (0, 1):
            got = arrived(t, j, h, 12)
            part[j, h, 0, k] = (part[j, h, 0, k].astype(F32) + got).astype(BF16)
            rcopy(t, j, h, part.at[j, h, 0, k], 13 + j, along(h, False, k)).start()

    def rs_final(t, j, h):
        carried = summed(t, j, h, 2) + arrived(t, j, h, 13) + arrived(t, j, h, 14)
        return em[t - 1, h, j].astype(F32) * carried

    def rs_sent(t):
        @pl.loop(0, 15)
        def _(msg):
            for j in (0, 1):
                for h in (0, 1):
                    rcopy(t, j, h, rs.at[t % 2, j, h, msg], msg, sib).wait_send()

    def keep(t, h, j, weighted):
        states_of(t)[row * 2 + h, j] = weighted.astype(BF16)
        ag_start(t, h, j)

    def each(fn, t):
        for h in (0, 1):
            for j in (0, 1):
                fn(t, h, j)

    def store_emitted(t):
        for h in (0, 1):
            value = e_final(t, h).astype(BF16)
            for j in (0, 1):
                em[t - 1, h, j] = value[:, j * HALF : (j + 1) * HALF]

    e_phase2(0)
    e_phase1(1)
    for h in (0, 1):
        first = e_final(0, h)
        for j in (0, 1):
            keep(0, h, j, first[:, j * HALF : (j + 1) * HALF])
    each(ag_relay1, 0)
    each(ag_relay2, 0)
    e_phase2(1)
    for i in range(4):
        blocks_copy(i).wait()
    each(ag_end, 0)

    for t in range(1, STEPS + 1):
        last = t == STEPS
        rs_first(t, 0)
        rs_direct(t, 0)
        rs_rest(t, 0)
        rs_merge(t, 0)
        rs_first(t, 1)
        rs_direct(t, 1)
        rs_rest(t, 1)
        rs_second(t, 0)
        rs_merge(t, 1)
        rs_merge2(t, 0)
        store_emitted(t)
        rs_second(t, 1)
        each(ag_sent, t - 1)
        total = jnp.zeros((SEQS, 1), F32)
        for j in (0, 1):
            if j == 1:
                rs_merge2(t, 1)
                if not last:
                    for h in (0, 1):
                        ag_relay1(t, h, 0)
            for h in (0, 1):
                weighted = rs_final(t, j, h)
                if last:
                    wfin[h, j] = weighted
                    total += jnp.sum(weighted, axis=1, keepdims=True)
                else:
                    keep(t, h, j, weighted)
        if not last:
            e_phase1(t + 1)
            for h in (0, 1):
                ag_relay2(t, h, 0)
            for h in (0, 1):
                ag_relay1(t, h, 1)
            for h in (0, 1):
                ag_relay2(t, h, 1)
            e_phase2(t + 1)
            rs_sent(t)
            each(ag_end, t)

    wide = iota((SEQS, 128), 0) == iota((SEQS, 128), 1)
    mine = jnp.sum(jnp.where(wide, total, 0.0), axis=0, keepdims=True)
    ar0[0] = jnp.broadcast_to(mine, (8, 128))
    ar1[row] = ar0[0]

    def a1(i):
        return remote(ar0.at[0], ar1.at[row], a_send.at[i - 1], a_recv.at[i - 1], row_peers[i - 1])

    def a2(i):
        return remote(ar0.at[1], ar2.at[col], a_send.at[6 + i], a_recv.at[6 + i], col_peers[i - 1])

    for i in range(1, 8):
        a1(i).start()
    for i in range(1, 8):
        a1(i).wait_recv()
    ar0[1] = jnp.sum(ar1[...], axis=0)
    ar2[col] = ar0[1]
    for i in range(1, 16):
        a2(i).start()
    for i in range(1, 16):
        a2(i).wait_recv()
    scale = jnp.sum(ar2[...], axis=0)[0:1] * (1.0 / STATES)
    log_ref[...] = jnp.log(scale)
    scale_col = jnp.sum(jnp.where(wide, scale, 0.0), axis=1, keepdims=True)
    for h in (0, 1):
        for j in (0, 1):
            post_ref[:, h * BLOCK + j * HALF : h * BLOCK + (j + 1) * HALF] = (wfin[h, j] / scale_col).astype(BF16)

    rs_sent(STEPS)
    for t in range(STEPS + 1):
        for h in (0, 1):
            for o in (1, 2, 3):
                e1(t, h, o).wait_send()
                e2(t, h, o).wait_send()
    for i in range(1, 8):
        a1(i).wait_send()
    for i in range(1, 16):
        a2(i).wait_send()


def on_device(blocks, source_ids, emission, tokens):
    vocab = emission.shape[0]
    dma = pltpu.SemaphoreType.DMA
    vmem = pltpu.VMEM
    posterior, logs = pl.pallas_call(
        kernel,
        out_shape=(jax.ShapeDtypeStruct((SEQS, 2 * BLOCK), BF16), jax.ShapeDtypeStruct((1, 128), F32)),
        in_specs=[
            pl.BlockSpec(memory_space=pltpu.SMEM),
            pl.BlockSpec(memory_space=pltpu.VMEM),
            pl.BlockSpec(memory_space=pl.ANY),
            pl.BlockSpec(memory_space=pl.ANY),
        ],
        out_specs=(pl.BlockSpec(memory_space=pltpu.VMEM), pl.BlockSpec(memory_space=pltpu.VMEM)),
        scratch_shapes=[
            vmem((32, BLOCK, BLOCK), BF16),
            vmem((32, vocab, BLOCK), BF16),
            vmem((4 * SLOT, vocab), BF16),
            vmem((STEPS + 1, 2, 3, 4, SLOT, BLOCK), BF16),
            vmem((STEPS + 1, 2, 4, 4, SLOT, BLOCK), BF16),
            vmem((STEPS + 1, 2, 4, 4, SLOT, BLOCK), BF16),
            vmem((STEPS, 2, 2, SEQS, HALF), BF16),
            vmem((16, 2, SEQS, HALF), BF16),
            vmem((16, 2, SEQS, HALF), BF16),
            vmem((2, 2, 4, 4, SEQS, HALF), BF16),
            vmem((2, 2, 2, 15, SEQS, HALF), BF16),
            vmem((2, 2, SEQS, HALF), F32),
            vmem((2, 8, 128), F32),
            vmem((8, 8, 128), F32),
            vmem((16, 8, 128), F32),
            dma((4,)),
            dma((32,)),
            dma((STEPS + 1, 2, 2, 3)),
            dma((STEPS + 1, 2, 2, 3)),
            dma((STEPS, 2, 2, 7)),
            dma((STEPS, 2, 2, 7)),
            dma((STEPS + 1, 2, 2, 15)),
            dma((STEPS + 1, 2, 2, 15)),
            dma((22,)),
            dma((22,)),
        ],
        compiler_params=pltpu.CompilerParams(
            collective_id=0, has_side_effects=True, vmem_limit_bytes=63 * 2**20
        ),
        name="forward",
    )(source_ids.reshape(-1), tokens, blocks.reshape(32, BLOCK, BLOCK), emission)
    return posterior, logs[0, :SEQS]


def solution(mesh):
    in_specs = (P("row", "col", None, None), P("row", "col"), P("col", "row"), P())
    out_specs = (P(None, ("row", "col")), P())
    return jax.shard_map(on_device, mesh=mesh, in_specs=in_specs, out_specs=out_specs, check_vma=False)
```

```python
import functools

import jax
import jax.numpy as jnp
from jax import lax
from jax.experimental import pallas as pl
from jax.experimental.pallas import tpu as pltpu
from jax.sharding import PartitionSpec as P

MESH = pl.DeviceIdType.MESH
STATES = 131072
SEQS = 104
CAP = 26
SLOT = 32
BLOCK = 512
STEPS = 3
ROWS = (slice(0, 48), slice(48, 104))
F32 = jnp.float32
BF16 = jnp.bfloat16


def iota(shape, dim):
    return lax.broadcasted_iota(jnp.int32, shape, dim).astype(F32)


def kernel(
    ids_ref, tok_ref, blocks_hbm, emis_hbm, post_ref, log_ref,
    blocks_v, emis_v, sel_v, pack, land1, land2, em, states_a, states_b, states_c, states_d, part_a, part_b, rs_a, rs_b, wfin, ar0, ar1, ar2,
    blk_sem, emis_sem, e_send, e_recv, ag_send, ag_recv, rs_send, rs_recv, a_send, a_recv,
):
    row = lax.axis_index("row")
    col = lax.axis_index("col")
    y, core = row // 2, row % 2
    x, z = col // 4, col % 4
    vocab = emis_v.shape[1]
    states = (states_a, states_b, states_c, states_d)
    part = (part_a, part_b)
    rs = (rs_a, rs_b)

    def at_plane(xd, zd):
        return (row, (xd % 4) * 4 + zd % 4)

    def along(h, first, off):
        if (h == 0) == first:
            return at_plane(x + off, z)
        return at_plane(x, z + off)

    def pq(h):
        return (x, z) if h == 0 else (z, x)

    def at_y(off):
        return (((y + off) % 4) * 2 + core, col)

    sib = (row + 1 - 2 * core, col)

    def remote(src, dst, ssem, rsem, dev):
        return pltpu.make_async_remote_copy(
            src_ref=src, dst_ref=dst, send_sem=ssem, recv_sem=rsem, device_id=dev, device_id_type=MESH
        )

    def emis_copy(chunk):
        return pltpu.make_async_copy(
            emis_hbm.at[:, pl.ds(pl.multiple_of(chunk * BLOCK, BLOCK), BLOCK)], emis_v.at[chunk], emis_sem.at[chunk]
        )

    def chunk_of(h, po, qd):
        p, _ = pq(h)
        pd = (p + po) % 4
        return (pd * 4 + qd) * 2 if h == 0 else (qd * 4 + pd) * 2 + 1

    for po in (2, 1, 3, 0):
        for h in (0, 1):
            @pl.loop(0, 4)
            def _(qd):
                emis_copy(chunk_of(h, po, qd)).start()

    def blocks_copy():
        return pltpu.make_async_copy(blocks_hbm, blocks_v, blk_sem)

    blocks_copy().start()

    barrier = pltpu.get_barrier_semaphore()
    row_peers = [(lax.rem(row + i, 8), col) for i in range(1, 8)]
    col_peers = [(row, lax.rem(col + i, 16)) for i in range(1, 16)]
    for dev in row_peers + col_peers:
        pl.semaphore_signal(barrier, inc=1, device_id=dev, device_id_type=MESH)

    eye = iota((SEQS, SEQS), 0) == iota((SEQS, SEQS), 1)
    before = iota((SEQS, SEQS), 0) < iota((SEQS, SEQS), 1)

    def to_col(v):
        return jnp.sum(jnp.where(eye, v, 0.0), axis=1, keepdims=True)

    def places(t):
        tok_row = tok_ref[t : t + 1, :].astype(F32)
        owner_row = jnp.zeros_like(tok_row)
        for k in range(1, 16):
            owner_row += jnp.where(tok_row >= float(k * vocab), 1.0, 0.0)
        owner_col = to_col(owner_row)
        same = jnp.where((owner_col == owner_row) & before, 1.0, 0.0)
        pos_row = jnp.sum(same, axis=0, keepdims=True)
        return tok_row, owner_row, owner_col, pos_row

    for t in range(STEPS + 1):
        tok_row, owner_row, owner_col, pos_row = places(t)
        me = col.astype(F32)
        slot_of = jnp.where((pos_row == iota((SLOT, SEQS), 0)) & (owner_row == me), 1.0, 0.0).astype(BF16)
        id_of = jnp.where(to_col(tok_row) - me * float(vocab) == iota((SEQS, vocab), 1), 1.0, 0.0).astype(BF16)
        sel_v[t * SLOT : (t + 1) * SLOT, :] = jnp.dot(slot_of, id_of, preferred_element_type=F32).astype(BF16)

    pl.semaphore_wait(barrier, 22)

    def e1(t, h, po):
        p, _ = pq(h)
        return remote(
            pack.at[t, h, po - 1], land1.at[t, h, :, p], e_send.at[t, 0], e_recv.at[t, 0, h],
            along(h, True, po),
        )

    def e2(t, h, qo):
        _, q = pq(h)
        return remote(
            land1.at[t, h, (q + qo) % 4], land2.at[t, h, q], e_send.at[t, 1], e_recv.at[t, 1, h],
            along(h, False, qo),
        )

    for po in (2, 1, 3, 0):
        for h in (0, 1):
            p, _ = pq(h)

            @pl.loop(0, 4)
            def _(qd):
                chunk = chunk_of(h, po, qd)
                emis_copy(chunk).wait()
                rows = jnp.dot(sel_v[...], emis_v[chunk], preferred_element_type=F32).astype(BF16)
                for t in range(STEPS + 1):
                    piece = rows[t * SLOT : (t + 1) * SLOT]
                    if po:
                        pack[t, h, po - 1, qd] = piece
                    else:
                        land1[t, h, qd, p] = piece

            if po:
                e1(0, h, po).start()

    def e_phase1(t):
        for po in (2, 1, 3):
            for h in (0, 1):
                e1(t, h, po).start()

    def e_phase2(t):
        for h in (0, 1):
            three = land1.at[t, h, :, 0:3]
            remote(three, three, e_send.at[t, 0], e_recv.at[t, 0, h], sib).wait_recv()
            for qo in (2, 1, 3):
                e2(t, h, qo).start()

    def e_final(t, h):
        p, q = pq(h)
        land2[t, h, q] = land1[t, h, q]
        _, _, owner_col, pos_row = places(t)
        if h == 0:
            high = jnp.zeros_like(owner_col)
            for k in range(1, 4):
                high += jnp.where(owner_col >= float(4 * k), 1.0, 0.0)
            place = (owner_col - 4.0 * high) * 4.0 + high
        else:
            place = owner_col
        target = place * float(SLOT) + to_col(pos_row)
        pick = jnp.where(iota((SEQS, 16 * SLOT), 1) == target, 1.0, 0.0).astype(BF16)
        three = land2.at[t, h, 0:3]
        remote(three, three, e_send.at[t, 1], e_recv.at[t, 1, h], sib).wait_recv()
        return jnp.dot(pick, land2[t, h].reshape(16 * SLOT, BLOCK), preferred_element_type=F32)

    def states_of(t, c):
        return states[c * 2 + t % 2]

    def ag(t, c, h, of_row, sem, dev):
        item = states_of(t, c).at[of_row * 2 + h]
        return remote(item, item, ag_send.at[c, h], ag_recv.at[t % 2, c, h, sem], dev)

    def same_core(off):
        return ((y + off) % 4) * 2 + core

    def ag_start(t, c, h):
        ag(t, c, h, row, 0, at_y(1)).start()
        ag(t, c, h, row, 1, at_y(3)).start()
        ag(t, c, h, row, 3, sib).start()

    def ag_relay1(t, c):
        for sem, off, on in ((0, 3, 1), (1, 1, 3)):
            for h in (0, 1):
                of = same_core(off)
                ag(t, c, h, of, sem, sib).wait_recv()
                if sem == h:
                    ag(t, c, h, of, 2, at_y(on)).start()
                ag(t, c, h, of, 3, sib).start()

    def ag_relay2(t, c):
        for h in (0, 1):
            of = same_core(2)
            ag(t, c, h, of, 2, sib).wait_recv()
            ag(t, c, h, of, 3, sib).start()

    def ag_end(t, c):
        for h in (0, 1):
            four = states_of(t, c).at[0:4]
            remote(four, four, ag_send.at[c, h], ag_recv.at[t % 2, c, h, 3], sib).wait_recv()

    def ag_sent(t, c):
        for h in (0, 1):
            seven = states_of(t, c).at[0:7]
            remote(seven, seven, ag_send.at[c, h], ag_recv.at[t % 2, c, h, 3], sib).wait_send()

    def product(t, c, h, po, k):
        p, q = pq(h)
        pd = (p + po) % 4
        qd = (q + 2 - k + 4) % 4
        dest = (pd * 4 + qd) * 2 if h == 0 else (qd * 4 + pd) * 2 + 1
        sid = ids_ref[dest]
        local = (sid // 32) * 2 + sid % 2
        acc = jnp.dot(states_of(t - 1, c)[local], blocks_v[dest], preferred_element_type=F32)
        part[c][h, po, k] = acc.astype(BF16)

    def rcopy(t, c, h, src, msg, sem, dev):
        return remote(src, rs[c].at[t % 2, h, msg], rs_send.at[c, h], rs_recv.at[t % 2, c, h, sem], dev)

    def arrived(t, c, h, k):
        rcopy(t, c, h, rs[c].at[t % 2, h, k], k, k, sib).wait_recv()
        return rs[c][t % 2, h, k].astype(F32)

    def both_arrived(t, c, h, msg, sem):
        pair = rs[c].at[t % 2, h, pl.ds(msg, 2)]
        remote(pair, pair, rs_send.at[c, h], rs_recv.at[t % 2, c, h, sem], sib).wait_recv()
        return rs[c][t % 2, h, msg].astype(F32) + rs[c][t % 2, h, msg + 1].astype(F32)

    def rs_multiply(t, c):
        @pl.loop(0, 2)
        def _(kk):
            for k in (2 * kk, 2 * kk + 1):
                for h in (0, 1):
                    product(t, c, h, 2, k)
            for k in (0, 1):
                for h in (0, 1):
                    rcopy(t, c, h, part[c].at[h, 2, 2 * kk + k], 2 * kk + k, 2 * kk + k, along(h, True, 1 + 2 * k)).start()

        @pl.loop(0, 2)
        def _(kk):
            for k in (0, 1):
                for h in (0, 1):
                    product(t, c, h, 3 - 2 * k, 2 * kk + k)
            for k in (0, 1):
                for h in (0, 1):
                    po = 3 - 2 * k
                    k2 = 2 * kk + k
                    rcopy(t, c, h, part[c].at[h, po, k2], 5 + 2 * k2 - k, 4 + k2, along(h, True, po)).start()

        @pl.loop(0, 2)
        def _(kk):
            for k in (0, 1):
                for h in (0, 1):
                    product(t, c, h, 1 + 2 * k, 2 * kk + k)

        @pl.loop(0, 2)
        def _(kk):
            for k in (0, 1):
                for h in (0, 1):
                    product(t, c, h, 0, 2 * kk + k)

    def rs_merge(t, c):
        @pl.loop(0, 2)
        def _(kk):
            for k in (0, 1):
                for h in (0, 1):
                    po = 1 + 2 * k
                    k2 = 2 * kk + k
                    got = arrived(t, c, h, k2)
                    part[c][h, po, k2] = (part[c][h, po, k2].astype(F32) + got).astype(BF16)
                    rcopy(t, c, h, part[c].at[h, po, k2], 4 + 2 * k2 + k, 4 + k2, along(h, True, po)).start()

    def summed(t, c, h, k):
        return part[c][h, 0, k].astype(F32) + both_arrived(t, c, h, 4 + 2 * k, 4 + k)

    def rs_second(t, c):
        for k in (0, 1, 3):
            for h in (0, 1):
                part[c][h, 0, k] = summed(t, c, h, k).astype(BF16)
                src = part[c].at[h, 0, k]
                if k == 0:
                    rcopy(t, c, h, src, 12, 8, along(h, False, 1 + 2 * c)).start()
                elif k == 1 and c == 1:
                    rcopy(t, c, h, src, 13, 9, along(h, False, 1)).start()
                elif k == 3 and c == 0:
                    rcopy(t, c, h, src, 14, 9, along(h, False, 3)).start()

    def rs_merge2(t, c):
        k = 1 if c == 0 else 3
        for h in (0, 1):
            rcopy(t, c, h, rs[c].at[t % 2, h, 12], 12, 8, sib).wait_recv()
            got = rs[c][t % 2, h, 12].astype(F32)
            part[c][h, 0, k] = (part[c][h, 0, k].astype(F32) + got).astype(BF16)
            rcopy(t, c, h, part[c].at[h, 0, k], 13 + c, 9, along(h, False, k)).start()

    def rs_final(t, c, h):
        carried = summed(t, c, h, 2) + both_arrived(t, c, h, 13, 9)
        return em[t - 1, h, ROWS[c]].astype(F32) * carried

    def rs_sent(t, c):
        for h in (0, 1):
            every = rs[c].at[t % 2, h]
            remote(every, every, rs_send.at[c, h], rs_recv.at[t % 2, c, h, 0], sib).wait_send()

    def keep(t, c, h, weighted):
        states_of(t, c)[row * 2 + h] = weighted.astype(BF16)
        ag_start(t, c, h)

    def finish(t, c):
        if t < STEPS:
            ag_sent(t - 1, c)
        for h in (0, 1):
            weighted = rs_final(t, c, h)
            if t == STEPS:
                wfin[h, ROWS[c]] = weighted
            else:
                keep(t, c, h, weighted)

    def begin(t, c):
        ag_end(t - 1, c)
        if t > 1:
            rs_sent(t - 1, c)
        rs_multiply(t, c)

    def store_emitted(t):
        for h in (0, 1):
            em[t - 1, h] = e_final(t, h).astype(BF16)

    e_phase2(0)
    e_phase1(1)
    for h in (0, 1):
        first = e_final(0, h)
        for c in (0, 1):
            keep(0, c, h, first[ROWS[c]])
    for c in (0, 1):
        ag_relay1(0, c)
    for c in (0, 1):
        ag_relay2(0, c)
    blocks_copy().wait()
    for t in range(1, STEPS + 1):
        begin(t, 0)
        if t > 1:
            finish(t - 1, 1)
        rs_merge(t, 0)
        if t > 1:
            ag_relay1(t - 1, 1)
        rs_second(t, 0)
        if t > 1:
            ag_relay2(t - 1, 1)
        e_phase2(t)
        rs_merge2(t, 0)
        begin(t, 1)
        store_emitted(t)
        finish(t, 0)
        rs_merge(t, 1)
        if t < STEPS:
            e_phase1(t + 1)
            ag_relay1(t, 0)
        rs_second(t, 1)
        if t < STEPS:
            ag_relay2(t, 0)
        rs_merge2(t, 1)
    finish(STEPS, 1)

    wide = iota((SEQS, 128), 0) == iota((SEQS, 128), 1)
    total = jnp.sum(wfin[0] + wfin[1], axis=1, keepdims=True)
    mine = jnp.sum(jnp.where(wide, total, 0.0), axis=0, keepdims=True)
    ar0[0] = jnp.broadcast_to(mine, (8, 128))
    ar1[row] = ar0[0]

    def a1(i):
        return remote(ar0.at[0], ar1.at[row], a_send.at[0], a_recv.at[0], row_peers[i - 1])

    def a2(i):
        return remote(ar0.at[1], ar2.at[col], a_send.at[1], a_recv.at[1], col_peers[i - 1])

    seven = remote(ar1.at[0:7], ar1.at[0:7], a_send.at[0], a_recv.at[0], sib)
    fifteen = remote(ar2.at[0:15], ar2.at[0:15], a_send.at[1], a_recv.at[1], sib)
    for i in range(1, 8):
        a1(i).start()
    seven.wait_recv()
    ar0[1] = jnp.sum(ar1[...], axis=0)
    ar2[col] = ar0[1]
    for i in range(1, 16):
        a2(i).start()
    fifteen.wait_recv()
    scale = jnp.sum(ar2[...], axis=0)[0:1] * (1.0 / STATES)
    log_ref[...] = jnp.log(scale)
    scale_col = jnp.sum(jnp.where(wide, scale, 0.0), axis=1, keepdims=True)
    for h in (0, 1):
        post_ref[:, h * BLOCK : (h + 1) * BLOCK] = (wfin[h] / scale_col).astype(BF16)

    for c in (0, 1):
        rs_sent(STEPS, c)
        ag_sent(STEPS - 1, c)
    for t in range(STEPS + 1):
        remote(pack.at[t], pack.at[t], e_send.at[t, 0], e_recv.at[t, 0, 0], sib).wait_send()
        remote(pack.at[t], pack.at[t], e_send.at[t, 1], e_recv.at[t, 0, 0], sib).wait_send()
    seven.wait_send()
    fifteen.wait_send()


def on_device(blocks, source_ids, emission, tokens):
    vocab = emission.shape[0]
    dma = pltpu.SemaphoreType.DMA
    vmem = pltpu.VMEM
    posterior, logs = pl.pallas_call(
        kernel,
        out_shape=(jax.ShapeDtypeStruct((SEQS, 2 * BLOCK), BF16), jax.ShapeDtypeStruct((1, 128), F32)),
        in_specs=[
            pl.BlockSpec(memory_space=pltpu.SMEM),
            pl.BlockSpec(memory_space=pltpu.VMEM),
            pl.BlockSpec(memory_space=pl.ANY),
            pl.BlockSpec(memory_space=pl.ANY),
        ],
        out_specs=(pl.BlockSpec(memory_space=pltpu.VMEM), pl.BlockSpec(memory_space=pltpu.VMEM)),
        scratch_shapes=[
            vmem((32, BLOCK, BLOCK), BF16),
            vmem((32, vocab, BLOCK), BF16),
            vmem((4 * SLOT, vocab), BF16),
            vmem((STEPS + 1, 2, 3, 4, SLOT, BLOCK), BF16),
            vmem((STEPS + 1, 2, 4, 4, SLOT, BLOCK), BF16),
            vmem((STEPS + 1, 2, 4, 4, SLOT, BLOCK), BF16),
            vmem((STEPS, 2, SEQS, BLOCK), BF16),
            vmem((16, 48, BLOCK), BF16),
            vmem((16, 48, BLOCK), BF16),
            vmem((16, 56, BLOCK), BF16),
            vmem((16, 56, BLOCK), BF16),
            vmem((2, 4, 4, 48, BLOCK), BF16),
            vmem((2, 4, 4, 56, BLOCK), BF16),
            vmem((2, 2, 15, 48, BLOCK), BF16),
            vmem((2, 2, 15, 56, BLOCK), BF16),
            vmem((2, SEQS, BLOCK), F32),
            vmem((2, 8, 128), F32),
            vmem((8, 8, 128), F32),
            vmem((16, 8, 128), F32),
            dma,
            dma((32,)),
            dma((STEPS + 1, 2)),
            dma((STEPS + 1, 2, 2)),
            dma((2, 2)),
            dma((2, 2, 2, 4)),
            dma((2, 2)),
            dma((2, 2, 2, 10)),
            dma((2,)),
            dma((2,)),
        ],
        compiler_params=pltpu.CompilerParams(
            collective_id=0, has_side_effects=True, vmem_limit_bytes=63 * 2**20
        ),
        name="forward",
    )(source_ids.reshape(-1), tokens, blocks.reshape(32, BLOCK, BLOCK), emission)
    return posterior, logs[0, :SEQS]


def solution(mesh):
    in_specs = (P("row", "col", None, None), P("row", "col"), P("col", "row"), P())
    out_specs = (P(None, ("row", "col")), P())
    return jax.shard_map(on_device, mesh=mesh, in_specs=in_specs, out_specs=out_specs, check_vma=False)
```

```python
import functools

import jax
import jax.numpy as jnp
from jax import lax
from jax.experimental import pallas as pl
from jax.experimental.pallas import tpu as pltpu
from jax.sharding import PartitionSpec as P

MESH = pl.DeviceIdType.MESH
STATES = 131072
SEQS = 104
CAP = 26
SLOT = 32
BLOCK = 512
STEPS = 3
ROWS = (slice(0, 48), slice(48, 104))
F32 = jnp.float32
BF16 = jnp.bfloat16


def iota(shape, dim):
    return lax.broadcasted_iota(jnp.int32, shape, dim).astype(F32)


def kernel(
    ids_ref, tok_ref, blocks_hbm, emis_hbm, wfin, scale_ref,
    blocks_v, emis_v, sel_v, pack, land1, land2, em, states_a, states_b, states_c, states_d, part_a, part_b, rs_a, rs_b, ar0, ar1, ar2,
    blk_sem, emis_sem, e_send, e_recv, ag_send, ag_recv, rs_send, rs_recv, a_send, a_recv,
):
    row = lax.axis_index("row")
    col = lax.axis_index("col")
    y, core = row // 2, row % 2
    x, z = col // 4, col % 4
    vocab = emis_v.shape[1]
    states = (states_a, states_b, states_c, states_d)
    part = (part_a, part_b)
    rs = (rs_a, rs_b)

    def at_plane(xd, zd):
        return (row, (xd % 4) * 4 + zd % 4)

    def along(h, first, off):
        if (h == 0) == first:
            return at_plane(x + off, z)
        return at_plane(x, z + off)

    def pq(h):
        return (x, z) if h == 0 else (z, x)

    def at_y(off):
        return (((y + off) % 4) * 2 + core, col)

    sib = (row + 1 - 2 * core, col)

    def remote(src, dst, ssem, rsem, dev):
        return pltpu.make_async_remote_copy(
            src_ref=src, dst_ref=dst, send_sem=ssem, recv_sem=rsem, device_id=dev, device_id_type=MESH
        )

    def emis_copy(chunk):
        return pltpu.make_async_copy(
            emis_hbm.at[:, pl.ds(pl.multiple_of(chunk * BLOCK, BLOCK), BLOCK)], emis_v.at[chunk], emis_sem.at[chunk]
        )

    def chunk_of(h, po, qd):
        p, _ = pq(h)
        pd = (p + po) % 4
        return (pd * 4 + qd) * 2 if h == 0 else (qd * 4 + pd) * 2 + 1

    for po in (2, 1, 3, 0):
        for h in (0, 1):
            @pl.loop(0, 4)
            def _(qd):
                emis_copy(chunk_of(h, po, qd)).start()

    def blocks_copy():
        return pltpu.make_async_copy(blocks_hbm, blocks_v, blk_sem)

    blocks_copy().start()

    barrier = pltpu.get_barrier_semaphore()
    row_peers = [(lax.rem(row + i, 8), col) for i in range(1, 8)]
    col_peers = [(row, lax.rem(col + i, 16)) for i in range(1, 16)]
    for dev in row_peers + col_peers:
        pl.semaphore_signal(barrier, inc=1, device_id=dev, device_id_type=MESH)

    eye = iota((SEQS, SEQS), 0) == iota((SEQS, SEQS), 1)
    before = iota((SEQS, SEQS), 0) < iota((SEQS, SEQS), 1)

    def to_col(v):
        return jnp.sum(jnp.where(eye, v, 0.0), axis=1, keepdims=True)

    def places(t):
        tok_row = tok_ref[t : t + 1, :].astype(F32)
        owner_row = jnp.zeros_like(tok_row)
        for k in range(1, 16):
            owner_row += jnp.where(tok_row >= float(k * vocab), 1.0, 0.0)
        owner_col = to_col(owner_row)
        same = jnp.where((owner_col == owner_row) & before, 1.0, 0.0)
        pos_row = jnp.sum(same, axis=0, keepdims=True)
        return tok_row, owner_row, owner_col, pos_row

    for t in range(STEPS + 1):
        tok_row, owner_row, owner_col, pos_row = places(t)
        me = col.astype(F32)
        slot_of = jnp.where((pos_row == iota((SLOT, SEQS), 0)) & (owner_row == me), 1.0, 0.0).astype(BF16)
        id_of = jnp.where(to_col(tok_row) - me * float(vocab) == iota((SEQS, vocab), 1), 1.0, 0.0).astype(BF16)
        sel_v[t * SLOT : (t + 1) * SLOT, :] = jnp.dot(slot_of, id_of, preferred_element_type=F32).astype(BF16)

    def e1(t, h, po):
        p, _ = pq(h)
        return remote(
            pack.at[t, h, po - 1], land1.at[t, h, :, p], e_send.at[t, 0], e_recv.at[t, 0, h],
            along(h, True, po),
        )

    def e2(t, h, qo):
        _, q = pq(h)
        return remote(
            land1.at[t, h, (q + qo) % 4], land2.at[t, h, q], e_send.at[t, 1], e_recv.at[t, 1, h],
            along(h, False, qo),
        )

    for po in (2, 1, 3, 0):
        for h in (0, 1):
            p, _ = pq(h)
            for qd in range(4):
                chunk = chunk_of(h, po, qd)
                emis_copy(chunk).wait()
                rows = jnp.dot(sel_v[...], emis_v[chunk], preferred_element_type=F32).astype(BF16)
                for t in range(STEPS + 1):
                    piece = rows[t * SLOT : (t + 1) * SLOT]
                    if po:
                        pack[t, h, po - 1, qd] = piece
                    else:
                        land1[t, h, qd, p] = piece
            if po == 2 and h == 0:
                pl.semaphore_wait(barrier, 22)
            if po:
                e1(0, h, po).start()

    def e_phase1(t):
        for po in (2, 1, 3):
            for h in (0, 1):
                e1(t, h, po).start()

    def e_phase2(t):
        for h in (0, 1):
            three = land1.at[t, h, :, 0:3]
            remote(three, three, e_send.at[t, 0], e_recv.at[t, 0, h], sib).wait_recv()
            for qo in (2, 1, 3):
                e2(t, h, qo).start()

    def e_final(t, h):
        p, q = pq(h)
        land2[t, h, q] = land1[t, h, q]
        _, _, owner_col, pos_row = places(t)
        if h == 0:
            high = jnp.zeros_like(owner_col)
            for k in range(1, 4):
                high += jnp.where(owner_col >= float(4 * k), 1.0, 0.0)
            place = (owner_col - 4.0 * high) * 4.0 + high
        else:
            place = owner_col
        target = place * float(SLOT) + to_col(pos_row)
        pick = jnp.where(iota((SEQS, 16 * SLOT), 1) == target, 1.0, 0.0).astype(BF16)
        three = land2.at[t, h, 0:3]
        remote(three, three, e_send.at[t, 1], e_recv.at[t, 1, h], sib).wait_recv()
        return jnp.dot(pick, land2[t, h].reshape(16 * SLOT, BLOCK), preferred_element_type=F32)

    def states_of(t, c):
        return states[c * 2 + t % 2]

    def ag(t, c, h, of_row, sem, dev):
        item = states_of(t, c).at[of_row * 2 + h]
        return remote(item, item, ag_send.at[c, h], ag_recv.at[t % 2, c, h, sem], dev)

    def same_core(off):
        return ((y + off) % 4) * 2 + core

    def ag_start(t, c, h):
        for sem, off in enumerate((1, 3, 2)):
            ag(t, c, h, row, sem, at_y(off)).start()
        ag(t, c, h, row, 3, sib).start()

    def ag_relay(t, c, sems):
        for sem in sems:
            for h in (0, 1):
                of = same_core((3, 1, 2)[sem])
                ag(t, c, h, of, sem, sib).wait_recv()
                ag(t, c, h, of, 3, sib).start()

    def ag_end(t, c):
        for h in (0, 1):
            four = states_of(t, c).at[0:4]
            remote(four, four, ag_send.at[c, h], ag_recv.at[t % 2, c, h, 3], sib).wait_recv()

    def ag_sent(t, c):
        for h in (0, 1):
            seven = states_of(t, c).at[0:7]
            remote(seven, seven, ag_send.at[c, h], ag_recv.at[t % 2, c, h, 3], sib).wait_send()

    def product(t, c, h, po, k):
        p, q = pq(h)
        pd = (p + po) % 4
        qd = (q + 2 - k + 4) % 4
        dest = (pd * 4 + qd) * 2 if h == 0 else (qd * 4 + pd) * 2 + 1
        sid = ids_ref[dest]
        local = (sid // 32) * 2 + sid % 2
        acc = jnp.dot(states_of(t - 1, c)[local], blocks_v[dest], preferred_element_type=F32)
        part[c][h, po, k] = acc.astype(BF16)

    def rcopy(t, c, h, src, msg, sem, dev):
        return remote(src, rs[c].at[t % 2, h, msg], rs_send.at[c, h], rs_recv.at[t % 2, c, h, sem], dev)

    def arrived(t, c, h, k):
        rcopy(t, c, h, rs[c].at[t % 2, h, k], k, k, sib).wait_recv()
        return rs[c][t % 2, h, k].astype(F32)

    def arrived_in(t, c, h, msg, count, sem):
        items = rs[c].at[t % 2, h, pl.ds(msg, count)]
        remote(items, items, rs_send.at[c, h], rs_recv.at[t % 2, c, h, sem], sib).wait_recv()
        return sum(rs[c][t % 2, h, msg + i].astype(F32) for i in range(count))

    def rs_multiply(t, c):
        @pl.loop(0, 2)
        def _(kk):
            for k in (2 * kk, 2 * kk + 1):
                for h in (0, 1):
                    product(t, c, h, 2, k)
            for k in (0, 1):
                for h in (0, 1):
                    rcopy(t, c, h, part[c].at[h, 2, 2 * kk + k], 2 * kk + k, 2 * kk + k, along(h, True, 1 + 2 * k)).start()

        @pl.loop(0, 2)
        def _(kk):
            for k in (0, 1):
                for h in (0, 1):
                    product(t, c, h, 3 - 2 * k, 2 * kk + k)
            for k in (0, 1):
                for h in (0, 1):
                    po = 3 - 2 * k
                    k2 = 2 * kk + k
                    rcopy(t, c, h, part[c].at[h, po, k2], 5 + 2 * k2 - k, 4 + k2, along(h, True, po)).start()

        @pl.loop(0, 2)
        def _(kk):
            for k in (0, 1):
                for h in (0, 1):
                    product(t, c, h, 1 + 2 * k, 2 * kk + k)

        @pl.loop(0, 2)
        def _(kk):
            for k in (0, 1):
                for h in (0, 1):
                    product(t, c, h, 0, 2 * kk + k)

    def rs_merge(t, c):
        @pl.loop(0, 2)
        def _(kk):
            for k in (0, 1):
                for h in (0, 1):
                    po = 1 + 2 * k
                    k2 = 2 * kk + k
                    got = arrived(t, c, h, k2)
                    part[c][h, po, k2] = (part[c][h, po, k2].astype(F32) + got).astype(BF16)
                    rcopy(t, c, h, part[c].at[h, po, k2], 4 + 2 * k2 + k, 4 + k2, along(h, True, po)).start()

    def summed(t, c, h, k):
        return part[c][h, 0, k].astype(F32) + arrived_in(t, c, h, 4 + 2 * k, 2, 4 + k)

    def rs_second(t, c):
        for k, msg, off in ((0, 12, 2), (1, 13, 1), (3, 14, 3)):
            for h in (0, 1):
                part[c][h, 0, k] = summed(t, c, h, k).astype(BF16)
                rcopy(t, c, h, part[c].at[h, 0, k], msg, 8, along(h, False, off)).start()

    def rs_final(t, c, h):
        carried = summed(t, c, h, 2) + arrived_in(t, c, h, 12, 3, 8)
        return em[t - 1, h, ROWS[c]].astype(F32) * carried

    def rs_sent(t, c):
        for h in (0, 1):
            every = rs[c].at[t % 2, h]
            remote(every, every, rs_send.at[c, h], rs_recv.at[t % 2, c, h, 0], sib).wait_send()

    def keep(t, c, h, weighted):
        states_of(t, c)[row * 2 + h] = weighted.astype(BF16)
        ag_start(t, c, h)

    def finish(t, c):
        if t < STEPS:
            ag_sent(t - 1, c)
        for h in (0, 1):
            weighted = rs_final(t, c, h)
            if t == STEPS:
                wfin[ROWS[c], h * BLOCK : (h + 1) * BLOCK] = weighted
            else:
                keep(t, c, h, weighted)

    def begin(t, c):
        ag_end(t - 1, c)
        if t > 1:
            rs_sent(t - 1, c)
        rs_multiply(t, c)

    def store_emitted(t):
        for h in (0, 1):
            em[t - 1, h] = e_final(t, h).astype(BF16)

    e_phase2(0)
    e_phase1(1)
    for h in (0, 1):
        first = e_final(0, h)
        for c in (0, 1):
            keep(0, c, h, first[ROWS[c]])
    for c in (0, 1):
        ag_relay(0, c, (0, 1, 2))
    blocks_copy().wait()
    for t in range(1, STEPS + 1):
        begin(t, 0)
        if t > 1:
            finish(t - 1, 1)
        rs_merge(t, 0)
        if t > 1:
            ag_relay(t - 1, 1, (0, 1))
        rs_second(t, 0)
        if t > 1:
            ag_relay(t - 1, 1, (2,))
        e_phase2(t)
        begin(t, 1)
        store_emitted(t)
        finish(t, 0)
        rs_merge(t, 1)
        if t < STEPS:
            e_phase1(t + 1)
            ag_relay(t, 0, (0, 1))
        rs_second(t, 1)
        if t < STEPS:
            ag_relay(t, 0, (2,))
    finish(STEPS, 1)

    wide = iota((SEQS, 128), 0) == iota((SEQS, 128), 1)
    total = jnp.sum(wfin[:, :BLOCK] + wfin[:, BLOCK:], axis=1, keepdims=True)
    mine = jnp.sum(jnp.where(wide, total, 0.0), axis=0, keepdims=True)
    ar0[0] = jnp.broadcast_to(mine, (8, 128))
    ar1[row] = ar0[0]

    def a1(i):
        return remote(ar0.at[0], ar1.at[row], a_send.at[0], a_recv.at[0], row_peers[i - 1])

    def a2(i):
        return remote(ar0.at[1], ar2.at[col], a_send.at[1], a_recv.at[1], col_peers[i - 1])

    seven = remote(ar1.at[0:7], ar1.at[0:7], a_send.at[0], a_recv.at[0], sib)
    fifteen = remote(ar2.at[0:15], ar2.at[0:15], a_send.at[1], a_recv.at[1], sib)
    for i in range(1, 8):
        a1(i).start()
    seven.wait_recv()
    ar0[1] = jnp.sum(ar1[...], axis=0)
    ar2[col] = ar0[1]
    for i in range(1, 16):
        a2(i).start()
    fifteen.wait_recv()
    scale_ref[...] = jnp.sum(ar2[...], axis=0) * (1.0 / STATES)

    for c in (0, 1):
        rs_sent(STEPS, c)
        ag_sent(STEPS - 1, c)
    for t in range(STEPS + 1):
        remote(pack.at[t], pack.at[t], e_send.at[t, 0], e_recv.at[t, 0, 0], sib).wait_send()
        remote(pack.at[t], pack.at[t], e_send.at[t, 1], e_recv.at[t, 0, 0], sib).wait_send()
    seven.wait_send()
    fifteen.wait_send()


def normalize(weights_ref, scale_ref, post_ref, log_ref):
    wide = iota((SEQS, 128), 0) == iota((SEQS, 128), 1)
    scale = scale_ref[0:1, :]
    log_ref[...] = jnp.log(scale[:, :SEQS])
    scale_col = jnp.sum(jnp.where(wide, scale, 0.0), axis=1, keepdims=True)
    post_ref[...] = (weights_ref[...] / scale_col).astype(BF16)


def on_device(blocks, source_ids, emission, tokens):
    vocab = emission.shape[0]
    dma = pltpu.SemaphoreType.DMA
    vmem = pltpu.VMEM
    weights, scale = pl.pallas_call(
        kernel,
        out_shape=(jax.ShapeDtypeStruct((SEQS, 2 * BLOCK), F32), jax.ShapeDtypeStruct((8, 128), F32)),
        in_specs=[
            pl.BlockSpec(memory_space=pltpu.SMEM),
            pl.BlockSpec(memory_space=pltpu.VMEM),
            pl.BlockSpec(memory_space=pl.ANY),
            pl.BlockSpec(memory_space=pl.ANY),
        ],
        out_specs=(pl.BlockSpec(memory_space=pltpu.VMEM), pl.BlockSpec(memory_space=pltpu.VMEM)),
        scratch_shapes=[
            vmem((32, BLOCK, BLOCK), BF16),
            vmem((32, vocab, BLOCK), BF16),
            vmem((4 * SLOT, vocab), BF16),
            vmem((STEPS + 1, 2, 3, 4, SLOT, BLOCK), BF16),
            vmem((STEPS + 1, 2, 4, 4, SLOT, BLOCK), BF16),
            vmem((STEPS + 1, 2, 4, 4, SLOT, BLOCK), BF16),
            vmem((STEPS, 2, SEQS, BLOCK), BF16),
            vmem((16, 48, BLOCK), BF16),
            vmem((16, 48, BLOCK), BF16),
            vmem((16, 56, BLOCK), BF16),
            vmem((16, 56, BLOCK), BF16),
            vmem((2, 4, 4, 48, BLOCK), BF16),
            vmem((2, 4, 4, 56, BLOCK), BF16),
            vmem((2, 2, 15, 48, BLOCK), BF16),
            vmem((2, 2, 15, 56, BLOCK), BF16),
            vmem((2, 8, 128), F32),
            vmem((8, 8, 128), F32),
            vmem((16, 8, 128), F32),
            dma,
            dma((32,)),
            dma((STEPS + 1, 2)),
            dma((STEPS + 1, 2, 2)),
            dma((2, 2)),
            dma((2, 2, 2, 4)),
            dma((2, 2)),
            dma((2, 2, 2, 9)),
            dma((2,)),
            dma((2,)),
        ],
        compiler_params=pltpu.CompilerParams(
            collective_id=0, has_side_effects=True, vmem_limit_bytes=63 * 2**20
        ),
        name="forward",
    )(source_ids.reshape(-1), tokens, blocks.reshape(32, BLOCK, BLOCK), emission)
    posterior, logs = pl.pallas_call(
        normalize,
        out_shape=(jax.ShapeDtypeStruct((SEQS, 2 * BLOCK), BF16), jax.ShapeDtypeStruct((1, SEQS), F32)),
        in_specs=[pl.BlockSpec(memory_space=pltpu.VMEM)] * 2,
        out_specs=(pl.BlockSpec(memory_space=pltpu.VMEM), pl.BlockSpec(memory_space=pltpu.VMEM)),
        name="normalize",
    )(weights, scale)
    return posterior, logs.reshape(SEQS)


def solution(mesh):
    in_specs = (P("row", "col", None, None), P("row", "col"), P("col", "row"), P())
    out_specs = (P(None, ("row", "col")), P())
    return jax.shard_map(on_device, mesh=mesh, in_specs=in_specs, out_specs=out_specs, check_vma=False)
```

```python
import functools

import jax
import jax.numpy as jnp
from jax import lax
from jax.experimental import pallas as pl
from jax.experimental.pallas import tpu as pltpu
from jax.sharding import PartitionSpec as P

MESH = pl.DeviceIdType.MESH
STATES = 131072
SEQS = 104
CAP = 26
SLOT = 32
BLOCK = 512
STEPS = 3
ROWS = (slice(0, 48), slice(48, 104))
F32 = jnp.float32
BF16 = jnp.bfloat16


def iota(shape, dim):
    return lax.broadcasted_iota(jnp.int32, shape, dim).astype(F32)


def kernel(
    ids_ref, tok_ref, blocks_hbm, emis_hbm, wfin, scale_ref,
    blocks_v, emis_v, sel_v, pack, land1, land2_a, land2_b, mid_a, mid_b, own, em, states_a, states_b, states_c, states_d, part_a, part_b, rs_a, rs_b, ar0, ar1, ar2,
    blk_sem, emis_sem, e_send, e_recv, e_send2, e_recv2, ag_send, ag_recv, rs_send, rs_recv, a_send, a_recv,
):
    row = lax.axis_index("row")
    col = lax.axis_index("col")
    y, core = row // 2, row % 2
    x, z = col // 4, col % 4
    vocab = emis_v.shape[1]
    states = (states_a, states_b, states_c, states_d)
    land2 = (land2_a, land2_b)
    mid = (mid_a, mid_b)
    part = (part_a, part_b)
    rs = (rs_a, rs_b)

    def at_plane(xd, zd):
        return (row, (xd % 4) * 4 + zd % 4)

    def along(h, first, off):
        if (h == 0) == first:
            return at_plane(x + off, z)
        return at_plane(x, z + off)

    def pq(h):
        return (x, z) if h == 0 else (z, x)

    def at_y(off):
        return (((y + off) % 4) * 2 + core, col)

    sib = (row + 1 - 2 * core, col)

    def remote(src, dst, ssem, rsem, dev):
        return pltpu.make_async_remote_copy(
            src_ref=src, dst_ref=dst, send_sem=ssem, recv_sem=rsem, device_id=dev, device_id_type=MESH
        )

    def emis_copy(chunk):
        return pltpu.make_async_copy(
            emis_hbm.at[:, pl.ds(pl.multiple_of(chunk * BLOCK, BLOCK), BLOCK)], emis_v.at[chunk], emis_sem.at[chunk]
        )

    def chunk_of(h, po, qd):
        p, _ = pq(h)
        pd = (p + po) % 4
        return (pd * 4 + qd) * 2 if h == 0 else (qd * 4 + pd) * 2 + 1

    for po in (2, 1, 3, 0):
        for h in (0, 1):
            @pl.loop(0, 4)
            def _(qd):
                emis_copy(chunk_of(h, po, qd)).start()

    def blocks_copy():
        return pltpu.make_async_copy(blocks_hbm, blocks_v, blk_sem)

    blocks_copy().start()

    barrier = pltpu.get_barrier_semaphore()
    row_peers = [(lax.rem(row + i, 8), col) for i in range(1, 8)]
    col_peers = [(row, lax.rem(col + i, 16)) for i in range(1, 16)]
    for dev in row_peers + col_peers:
        pl.semaphore_signal(barrier, inc=1, device_id=dev, device_id_type=MESH)

    eye = iota((SEQS, SEQS), 0) == iota((SEQS, SEQS), 1)
    before = iota((SEQS, SEQS), 0) < iota((SEQS, SEQS), 1)

    def to_col(v):
        return jnp.sum(jnp.where(eye, v, 0.0), axis=1, keepdims=True)

    def places(t):
        tok_row = tok_ref[t : t + 1, :].astype(F32)
        owner_row = jnp.zeros_like(tok_row)
        for k in range(1, 16):
            owner_row += jnp.where(tok_row >= float(k * vocab), 1.0, 0.0)
        owner_col = to_col(owner_row)
        same = jnp.where((owner_col == owner_row) & before, 1.0, 0.0)
        pos_row = jnp.sum(same, axis=0, keepdims=True)
        return tok_row, owner_row, owner_col, pos_row

    for t in range(STEPS + 1):
        tok_row, owner_row, owner_col, pos_row = places(t)
        me = col.astype(F32)
        slot_of = jnp.where((pos_row == iota((SLOT, SEQS), 0)) & (owner_row == me), 1.0, 0.0).astype(BF16)
        id_of = jnp.where(to_col(tok_row) - me * float(vocab) == iota((SEQS, vocab), 1), 1.0, 0.0).astype(BF16)
        sel_v[t * SLOT : (t + 1) * SLOT, :] = jnp.dot(slot_of, id_of, preferred_element_type=F32).astype(BF16)

    def e1(t, h, po):
        p, _ = pq(h)
        return remote(
            pack.at[t, h, po - 1], land1.at[t, h, :, p], e_send.at[t], e_recv.at[t, h],
            along(h, True, po),
        )

    def e2(t, c, h, qo):
        return remote(
            mid[c].at[h, qo - 1], land2[c].at[t, h, qo - 1], e_send2.at[c], e_recv2.at[t, c, h], along(h, False, qo)
        )

    for po in (2, 1, 3, 0):
        for h in (0, 1):
            p, _ = pq(h)
            for qd in range(4):
                chunk = chunk_of(h, po, qd)
                emis_copy(chunk).wait()
                rows = jnp.dot(sel_v[...], emis_v[chunk], preferred_element_type=F32).astype(BF16)
                for t in range(STEPS + 1):
                    piece = rows[t * SLOT : (t + 1) * SLOT]
                    if po:
                        pack[t, h, po - 1, qd] = piece
                    else:
                        land1[t, h, qd, p] = piece
            if po == 2 and h == 0:
                pl.semaphore_wait(barrier, 22)
            if po:
                e1(0, h, po).start()

    def e_first(t, po):
        for h in (0, 1):
            e1(t, h, po).start()

    def e_sent2():
        for c in (0, 1):
            remote(mid[c], mid[c], e_send2.at[c], e_recv2.at[0, c, 0], sib).wait_send()

    def e_middle(t, h):
        _, q = pq(h)
        _, _, owner_col, pos_row = places(t)
        x_of = jnp.zeros_like(owner_col)
        for k in range(1, 4):
            x_of += jnp.where(owner_col >= float(4 * k), 1.0, 0.0)
        z_of = owner_col - 4.0 * x_of
        p_of, q_of = (x_of, z_of) if h == 0 else (z_of, x_of)
        place = p_of * float(SLOT) + to_col(pos_row)
        lane = iota((SEQS, 4 * SLOT), 1)
        pick = jnp.where((lane == place) & (q_of == q.astype(F32)), 1.0, 0.0).astype(BF16)
        three = land1.at[t, h, :, 0:3]
        remote(three, three, e_send.at[t], e_recv.at[t, h], sib).wait_recv()
        for qo in (2, 1, 3, 0):
            packed = land1[t, h, (q + qo) % 4].reshape(4 * SLOT, BLOCK)
            rows = jnp.dot(pick, packed, preferred_element_type=F32).astype(BF16)
            if qo:
                for c in (0, 1):
                    mid[c][h, qo - 1] = rows[ROWS[c]]
            else:
                own[h] = rows

    def e_second(t, c, h):
        for qo in (2, 1, 3):
            e2(t, c, h, qo).start()

    def e_final(t, c, h):
        three = land2[c].at[t, h]
        remote(three, three, e_send2.at[c], e_recv2.at[t, c, h], sib).wait_recv()
        return own[h, ROWS[c]].astype(F32) + sum(land2[c][t, h, i].astype(F32) for i in range(3))

    def states_of(t, c):
        return states[c * 2 + t % 2]

    def ag(t, c, h, of_row, sem, dev):
        item = states_of(t, c).at[of_row * 2 + h]
        return remote(item, item, ag_send.at[c, h], ag_recv.at[t % 2, c, h, sem], dev)

    def same_core(off):
        return ((y + off) % 4) * 2 + core

    def ag_start(t, c, h):
        for sem, off in enumerate((1, 3, 2)):
            ag(t, c, h, row, sem, at_y(off)).start()
        ag(t, c, h, row, 3, sib).start()

    def ag_relay(t, c, sems):
        for sem in sems:
            for h in (0, 1):
                of = same_core((3, 1, 2)[sem])
                ag(t, c, h, of, sem, sib).wait_recv()
                ag(t, c, h, of, 3, sib).start()

    def ag_end(t, c):
        for h in (0, 1):
            four = states_of(t, c).at[0:4]
            remote(four, four, ag_send.at[c, h], ag_recv.at[t % 2, c, h, 3], sib).wait_recv()

    def ag_sent(t, c):
        for h in (0, 1):
            seven = states_of(t, c).at[0:7]
            remote(seven, seven, ag_send.at[c, h], ag_recv.at[t % 2, c, h, 3], sib).wait_send()

    def product(t, c, h, po, k):
        p, q = pq(h)
        pd = (p + po) % 4
        qd = (q + 2 - k + 4) % 4
        dest = (pd * 4 + qd) * 2 if h == 0 else (qd * 4 + pd) * 2 + 1
        sid = ids_ref[dest]
        local = (sid // 32) * 2 + sid % 2
        acc = jnp.dot(states_of(t - 1, c)[local], blocks_v[dest], preferred_element_type=F32)
        part[c][h, po, k] = acc.astype(BF16)

    def rcopy(t, c, h, src, msg, sem, dev):
        return remote(src, rs[c].at[t % 2, h, msg], rs_send.at[c, h], rs_recv.at[t % 2, c, h, sem], dev)

    def arrived(t, c, h, k):
        rcopy(t, c, h, rs[c].at[t % 2, h, k], k, k, sib).wait_recv()
        return rs[c][t % 2, h, k].astype(F32)

    def arrived_in(t, c, h, msg, count, sem):
        items = rs[c].at[t % 2, h, pl.ds(msg, count)]
        remote(items, items, rs_send.at[c, h], rs_recv.at[t % 2, c, h, sem], sib).wait_recv()
        return sum(rs[c][t % 2, h, msg + i].astype(F32) for i in range(count))

    def rs_multiply(t, c):
        @pl.loop(0, 2)
        def _(kk):
            for k in (2 * kk, 2 * kk + 1):
                for h in (0, 1):
                    product(t, c, h, 2, k)
            for k in (0, 1):
                for h in (0, 1):
                    rcopy(t, c, h, part[c].at[h, 2, 2 * kk + k], 2 * kk + k, 2 * kk + k, along(h, True, 1 + 2 * k)).start()

        @pl.loop(0, 2)
        def _(kk):
            for k in (0, 1):
                for h in (0, 1):
                    product(t, c, h, 3 - 2 * k, 2 * kk + k)
            for k in (0, 1):
                for h in (0, 1):
                    po = 3 - 2 * k
                    k2 = 2 * kk + k
                    rcopy(t, c, h, part[c].at[h, po, k2], 5 + 2 * k2 - k, 4 + k2, along(h, True, po)).start()

        @pl.loop(0, 2)
        def _(kk):
            for k in (0, 1):
                for h in (0, 1):
                    product(t, c, h, 1 + 2 * k, 2 * kk + k)

        @pl.loop(0, 2)
        def _(kk):
            for k in (0, 1):
                for h in (0, 1):
                    product(t, c, h, 0, 2 * kk + k)

    def rs_merge(t, c):
        @pl.loop(0, 2)
        def _(kk):
            for k in (0, 1):
                for h in (0, 1):
                    po = 1 + 2 * k
                    k2 = 2 * kk + k
                    got = arrived(t, c, h, k2)
                    part[c][h, po, k2] = (part[c][h, po, k2].astype(F32) + got).astype(BF16)
                    rcopy(t, c, h, part[c].at[h, po, k2], 4 + 2 * k2 + k, 4 + k2, along(h, True, po)).start()

    def summed(t, c, h, k):
        return part[c][h, 0, k].astype(F32) + arrived_in(t, c, h, 4 + 2 * k, 2, 4 + k)

    def rs_second(t, c):
        for k, msg, off in ((0, 12, 2), (1, 13, 1), (3, 14, 3)):
            for h in (0, 1):
                part[c][h, 0, k] = summed(t, c, h, k).astype(BF16)
                rcopy(t, c, h, part[c].at[h, 0, k], msg, 8, along(h, False, off)).start()

    def rs_final(t, c, h):
        carried = summed(t, c, h, 2) + arrived_in(t, c, h, 12, 3, 8)
        return em[t - 1, h, ROWS[c]].astype(F32) * carried

    def rs_sent(t, c):
        for h in (0, 1):
            every = rs[c].at[t % 2, h]
            remote(every, every, rs_send.at[c, h], rs_recv.at[t % 2, c, h, 0], sib).wait_send()

    def keep(t, c, h, weighted):
        states_of(t, c)[row * 2 + h] = weighted.astype(BF16)
        ag_start(t, c, h)

    def finish(t, c):
        if t < STEPS:
            ag_sent(t - 1, c)
        for h in (0, 1):
            weighted = rs_final(t, c, h)
            if t == STEPS:
                wfin[ROWS[c], h * BLOCK : (h + 1) * BLOCK] = weighted
            else:
                keep(t, c, h, weighted)

    def begin(t, c):
        ag_end(t - 1, c)
        if t > 1:
            rs_sent(t - 1, c)
        rs_multiply(t, c)

    def store_emitted(t, c):
        for h in (0, 1):
            em[t - 1, h, ROWS[c]] = e_final(t, c, h).astype(BF16)

    for h in (0, 1):
        e_middle(0, h)
        e_second(0, 0, h)
    for h in (0, 1):
        e_second(0, 1, h)
    for po in (2, 1, 3):
        e_first(1, po)
    for c in (0, 1):
        for h in (0, 1):
            keep(0, c, h, e_final(0, c, h))
    for c in (0, 1):
        ag_relay(0, c, (0, 1, 2))
    e_sent2()
    for h in (0, 1):
        e_middle(1, h)
    blocks_copy().wait()

    def emission(t, slot):
        if t == STEPS:
            return
        if slot < 3:
            e_first(t + 1, (2, 1, 3)[slot])
        elif slot == 3:
            e_sent2()
            e_middle(t + 1, 0)
            e_second(t + 1, 0, 0)
        elif slot == 4:
            e_middle(t + 1, 1)
            e_second(t + 1, 0, 1)
        else:
            for h in (0, 1):
                e_second(t + 1, 1, h)

    for t in range(1, STEPS + 1):
        begin(t, 0)
        if t == 1:
            for c in (0, 1):
                for h in (0, 1):
                    e_second(1, c, h)
        if t > 1:
            finish(t - 1, 1)
        rs_merge(t, 0)
        if t > 1:
            ag_relay(t - 1, 1, (0, 1))
        rs_second(t, 0)
        if t > 1:
            ag_relay(t - 1, 1, (2,))
        begin(t, 1)
        emission(t, 0)
        emission(t, 1)
        emission(t, 2)
        store_emitted(t, 0)
        store_emitted(t, 1)
        finish(t, 0)
        rs_merge(t, 1)
        if t < STEPS:
            ag_relay(t, 0, (0, 1))
        rs_second(t, 1)
        emission(t, 3)
        emission(t, 4)
        emission(t, 5)
        if t < STEPS:
            ag_relay(t, 0, (2,))
    finish(STEPS, 1)

    wide = iota((SEQS, 128), 0) == iota((SEQS, 128), 1)
    total = jnp.sum(wfin[:, :BLOCK] + wfin[:, BLOCK:], axis=1, keepdims=True)
    mine = jnp.sum(jnp.where(wide, total, 0.0), axis=0, keepdims=True)
    ar0[0] = jnp.broadcast_to(mine, (8, 128))
    ar1[row] = ar0[0]

    def a1(i):
        return remote(ar0.at[0], ar1.at[row], a_send.at[0], a_recv.at[0], row_peers[i - 1])

    def a2(i):
        return remote(ar0.at[1], ar2.at[col], a_send.at[1], a_recv.at[1], col_peers[i - 1])

    seven = remote(ar1.at[0:7], ar1.at[0:7], a_send.at[0], a_recv.at[0], sib)
    fifteen = remote(ar2.at[0:15], ar2.at[0:15], a_send.at[1], a_recv.at[1], sib)
    for i in range(1, 8):
        a1(i).start()
    seven.wait_recv()
    ar0[1] = jnp.sum(ar1[...], axis=0)
    ar2[col] = ar0[1]
    for i in range(1, 16):
        a2(i).start()
    fifteen.wait_recv()
    scale_ref[...] = jnp.sum(ar2[...], axis=0) * (1.0 / STATES)

    for c in (0, 1):
        rs_sent(STEPS, c)
        ag_sent(STEPS - 1, c)
    e_sent2()
    for t in range(STEPS + 1):
        remote(pack.at[t], pack.at[t], e_send.at[t], e_recv.at[t, 0], sib).wait_send()
    seven.wait_send()
    fifteen.wait_send()


def normalize(weights_ref, scale_ref, post_ref, log_ref):
    wide = iota((SEQS, 128), 0) == iota((SEQS, 128), 1)
    scale = scale_ref[0:1, :]
    log_ref[...] = jnp.log(scale[:, :SEQS])
    scale_col = jnp.sum(jnp.where(wide, scale, 0.0), axis=1, keepdims=True)
    post_ref[...] = (weights_ref[...] / scale_col).astype(BF16)


def on_device(blocks, source_ids, emission, tokens):
    vocab = emission.shape[0]
    dma = pltpu.SemaphoreType.DMA
    vmem = pltpu.VMEM
    weights, scale = pl.pallas_call(
        kernel,
        out_shape=(jax.ShapeDtypeStruct((SEQS, 2 * BLOCK), F32), jax.ShapeDtypeStruct((8, 128), F32)),
        in_specs=[
            pl.BlockSpec(memory_space=pltpu.SMEM),
            pl.BlockSpec(memory_space=pltpu.VMEM),
            pl.BlockSpec(memory_space=pl.ANY),
            pl.BlockSpec(memory_space=pl.ANY),
        ],
        out_specs=(pl.BlockSpec(memory_space=pltpu.VMEM), pl.BlockSpec(memory_space=pltpu.VMEM)),
        scratch_shapes=[
            vmem((32, BLOCK, BLOCK), BF16),
            vmem((32, vocab, BLOCK), BF16),
            vmem((4 * SLOT, vocab), BF16),
            vmem((STEPS + 1, 2, 3, 4, SLOT, BLOCK), BF16),
            vmem((STEPS + 1, 2, 4, 4, SLOT, BLOCK), BF16),
            vmem((STEPS + 1, 2, 3, 48, BLOCK), BF16),
            vmem((STEPS + 1, 2, 3, 56, BLOCK), BF16),
            vmem((2, 3, 48, BLOCK), BF16),
            vmem((2, 3, 56, BLOCK), BF16),
            vmem((2, SEQS, BLOCK), BF16),
            vmem((STEPS, 2, SEQS, BLOCK), BF16),
            vmem((16, 48, BLOCK), BF16),
            vmem((16, 48, BLOCK), BF16),
            vmem((16, 56, BLOCK), BF16),
            vmem((16, 56, BLOCK), BF16),
            vmem((2, 4, 4, 48, BLOCK), BF16),
            vmem((2, 4, 4, 56, BLOCK), BF16),
            vmem((2, 2, 15, 48, BLOCK), BF16),
            vmem((2, 2, 15, 56, BLOCK), BF16),
            vmem((2, 8, 128), F32),
            vmem((8, 8, 128), F32),
            vmem((16, 8, 128), F32),
            dma,
            dma((32,)),
            dma((STEPS + 1,)),
            dma((STEPS + 1, 2)),
            dma((2,)),
            dma((STEPS + 1, 2, 2)),
            dma((2, 2)),
            dma((2, 2, 2, 4)),
            dma((2, 2)),
            dma((2, 2, 2, 9)),
            dma((2,)),
            dma((2,)),
        ],
        compiler_params=pltpu.CompilerParams(
            collective_id=0, has_side_effects=True, vmem_limit_bytes=63 * 2**20
        ),
        name="forward",
    )(source_ids.reshape(-1), tokens, blocks.reshape(32, BLOCK, BLOCK), emission)
    posterior, logs = pl.pallas_call(
        normalize,
        out_shape=(jax.ShapeDtypeStruct((SEQS, 2 * BLOCK), BF16), jax.ShapeDtypeStruct((1, SEQS), F32)),
        in_specs=[pl.BlockSpec(memory_space=pltpu.VMEM)] * 2,
        out_specs=(pl.BlockSpec(memory_space=pltpu.VMEM), pl.BlockSpec(memory_space=pltpu.VMEM)),
        name="normalize",
    )(weights, scale)
    return posterior, logs.reshape(SEQS)


def solution(mesh):
    in_specs = (P("row", "col", None, None), P("row", "col"), P("col", "row"), P())
    out_specs = (P(None, ("row", "col")), P())
    return jax.shard_map(on_device, mesh=mesh, in_specs=in_specs, out_specs=out_specs, check_vma=False)
```

```python
import functools

import jax
import jax.numpy as jnp
from jax import lax
from jax.experimental import pallas as pl
from jax.experimental.pallas import tpu as pltpu
from jax.sharding import PartitionSpec as P

MESH = pl.DeviceIdType.MESH
STATES = 131072
SEQS = 104
CAP = 26
SLOT = 32
BLOCK = 512
STEPS = 3
ROWS = (slice(0, 48), slice(48, 104))
F32 = jnp.float32
BF16 = jnp.bfloat16


def iota(shape, dim):
    return lax.broadcasted_iota(jnp.int32, shape, dim).astype(F32)


def kernel(
    ids_ref, tok_ref, blocks_hbm, emis_hbm, wfin, scale_ref,
    blocks_v, emis_v, sel_v, pack, land1, land2_a, land2_b, mid_a, mid_b, own, em, states_a, states_b, states_c, states_d, part_a, part_b, rs_a, rs_b, ar0, ar1, ar2,
    blk_sem, emis_sem, e_send, e_recv, e_send2, e_recv2, ag_send, ag_recv, rs_send, rs_recv, a_send, a_recv,
):
    row = lax.axis_index("row")
    col = lax.axis_index("col")
    y, core = row // 2, row % 2
    x, z = col // 4, col % 4
    vocab = emis_v.shape[1]
    states = (states_a, states_b, states_c, states_d)
    land2 = (land2_a, land2_b)
    mid = (mid_a, mid_b)
    part = (part_a, part_b)
    rs = (rs_a, rs_b)

    def at_plane(xd, zd):
        return (row, (xd % 4) * 4 + zd % 4)

    def along(h, first, off):
        if (h == 0) == first:
            return at_plane(x + off, z)
        return at_plane(x, z + off)

    def pq(h):
        return (x, z) if h == 0 else (z, x)

    def at_y(off):
        return (((y + off) % 4) * 2 + core, col)

    sib = (row + 1 - 2 * core, col)

    def remote(src, dst, ssem, rsem, dev):
        return pltpu.make_async_remote_copy(
            src_ref=src, dst_ref=dst, send_sem=ssem, recv_sem=rsem, device_id=dev, device_id_type=MESH
        )

    def emis_copy(chunk):
        return pltpu.make_async_copy(
            emis_hbm.at[:, pl.ds(pl.multiple_of(chunk * BLOCK, BLOCK), BLOCK)], emis_v.at[chunk], emis_sem.at[chunk]
        )

    def chunk_of(h, po, qd):
        p, _ = pq(h)
        pd = (p + po) % 4
        return (pd * 4 + qd) * 2 if h == 0 else (qd * 4 + pd) * 2 + 1

    for po in (2, 1, 3, 0):
        for h in (0, 1):
            @pl.loop(0, 4)
            def _(qd):
                emis_copy(chunk_of(h, po, qd)).start()

    def blocks_copy():
        return pltpu.make_async_copy(blocks_hbm, blocks_v, blk_sem)

    blocks_copy().start()

    barrier = pltpu.get_barrier_semaphore()
    row_peers = [(lax.rem(row + i, 8), col) for i in range(1, 8)]
    col_peers = [(row, lax.rem(col + i, 16)) for i in range(1, 16)]
    for dev in row_peers + col_peers:
        pl.semaphore_signal(barrier, inc=1, device_id=dev, device_id_type=MESH)

    eye = iota((SEQS, SEQS), 0) == iota((SEQS, SEQS), 1)
    before = iota((SEQS, SEQS), 0) < iota((SEQS, SEQS), 1)

    def to_col(v):
        return jnp.sum(jnp.where(eye, v, 0.0), axis=1, keepdims=True)

    def places(t):
        tok_row = tok_ref[t : t + 1, :].astype(F32)
        owner_row = jnp.zeros_like(tok_row)
        for k in range(1, 16):
            owner_row += jnp.where(tok_row >= float(k * vocab), 1.0, 0.0)
        owner_col = to_col(owner_row)
        same = jnp.where((owner_col == owner_row) & before, 1.0, 0.0)
        pos_row = jnp.sum(same, axis=0, keepdims=True)
        return tok_row, owner_row, owner_col, pos_row

    for t in range(STEPS + 1):
        tok_row, owner_row, owner_col, pos_row = places(t)
        me = col.astype(F32)
        slot_of = jnp.where((pos_row == iota((SLOT, SEQS), 0)) & (owner_row == me), 1.0, 0.0).astype(BF16)
        id_of = jnp.where(to_col(tok_row) - me * float(vocab) == iota((SEQS, vocab), 1), 1.0, 0.0).astype(BF16)
        sel_v[t * SLOT : (t + 1) * SLOT, :] = jnp.dot(slot_of, id_of, preferred_element_type=F32).astype(BF16)

    def e1(t, h, po):
        p, _ = pq(h)
        return remote(
            pack.at[t, h, po - 1], land1.at[t, h, :, p], e_send.at[t], e_recv.at[t, h],
            along(h, True, po),
        )

    def e2(t, c, h, qo):
        return remote(
            mid[c].at[h, qo - 1], land2[c].at[t, h, qo - 1], e_send2.at[c], e_recv2.at[t, c, h], along(h, False, qo)
        )

    for po in (2, 1, 3, 0):
        for h in (0, 1):
            p, _ = pq(h)
            for qd in range(4):
                chunk = chunk_of(h, po, qd)
                emis_copy(chunk).wait()
                rows = jnp.dot(sel_v[...], emis_v[chunk], preferred_element_type=F32).astype(BF16)
                for t in range(STEPS + 1):
                    piece = rows[t * SLOT : (t + 1) * SLOT]
                    if po:
                        pack[t, h, po - 1, qd] = piece
                    else:
                        land1[t, h, qd, p] = piece
            if po == 2 and h == 0:
                pl.semaphore_wait(barrier, 22)
            if po:
                e1(0, h, po).start()

    def e_first(t, po):
        for h in (0, 1):
            e1(t, h, po).start()

    def e_sent2():
        for c in (0, 1):
            remote(mid[c], mid[c], e_send2.at[c], e_recv2.at[0, c, 0], sib).wait_send()

    def e_middle(t, h):
        _, q = pq(h)
        _, _, owner_col, pos_row = places(t)
        x_of = jnp.zeros_like(owner_col)
        for k in range(1, 4):
            x_of += jnp.where(owner_col >= float(4 * k), 1.0, 0.0)
        z_of = owner_col - 4.0 * x_of
        p_of, q_of = (x_of, z_of) if h == 0 else (z_of, x_of)
        place = p_of * float(SLOT) + to_col(pos_row)
        lane = iota((SEQS, 4 * SLOT), 1)
        pick = jnp.where((lane == place) & (q_of == q.astype(F32)), 1.0, 0.0).astype(BF16)
        three = land1.at[t, h, :, 0:3]
        remote(three, three, e_send.at[t], e_recv.at[t, h], sib).wait_recv()
        for qo in (2, 1, 3, 0):
            packed = land1[t, h, (q + qo) % 4].reshape(4 * SLOT, BLOCK)
            rows = jnp.dot(pick, packed, preferred_element_type=F32).astype(BF16)
            if qo:
                for c in (0, 1):
                    mid[c][h, qo - 1] = rows[ROWS[c]]
            else:
                own[h] = rows

    def e_second(t, c, h):
        for qo in (2, 1, 3):
            e2(t, c, h, qo).start()

    def e_final(t, c, h):
        three = land2[c].at[t, h]
        remote(three, three, e_send2.at[c], e_recv2.at[t, c, h], sib).wait_recv()
        return own[h, ROWS[c]].astype(F32) + sum(land2[c][t, h, i].astype(F32) for i in range(3))

    def states_of(t, c):
        return states[c * 2 + t % 2]

    def ag(t, c, h, of_row, sem, dev):
        item = states_of(t, c).at[of_row * 2 + h]
        return remote(item, item, ag_send.at[c, h], ag_recv.at[t % 2, c, h, sem], dev)

    def same_core(off):
        return ((y + off) % 4) * 2 + core

    def ag_start(t, c, h):
        for sem, off in enumerate((1, 3, 2)):
            ag(t, c, h, row, sem, at_y(off)).start()
        ag(t, c, h, row, 3, sib).start()

    def ag_relay(t, c, sems):
        for sem in sems:
            for h in (0, 1):
                of = same_core((3, 1, 2)[sem])
                ag(t, c, h, of, sem, sib).wait_recv()
                ag(t, c, h, of, 3, sib).start()

    def ag_end(t, c):
        for h in (0, 1):
            four = states_of(t, c).at[0:4]
            remote(four, four, ag_send.at[c, h], ag_recv.at[t % 2, c, h, 3], sib).wait_recv()

    def ag_sent(t, c):
        for h in (0, 1):
            seven = states_of(t, c).at[0:7]
            remote(seven, seven, ag_send.at[c, h], ag_recv.at[t % 2, c, h, 3], sib).wait_send()

    def product(t, c, h, po, k):
        p, q = pq(h)
        pd = (p + po) % 4
        qd = (q + 2 - k + 4) % 4
        dest = (pd * 4 + qd) * 2 if h == 0 else (qd * 4 + pd) * 2 + 1
        sid = ids_ref[dest]
        local = (sid // 32) * 2 + sid % 2
        acc = jnp.dot(states_of(t - 1, c)[local], blocks_v[dest], preferred_element_type=F32)
        part[c][h, po, k] = acc.astype(BF16)

    def rcopy(t, c, h, src, msg, sem, dev):
        return remote(src, rs[c].at[t % 2, h, msg], rs_send.at[c, h], rs_recv.at[t % 2, c, h, sem], dev)

    def arrived(t, c, h, k):
        rcopy(t, c, h, rs[c].at[t % 2, h, k], k, k, sib).wait_recv()
        return rs[c][t % 2, h, k].astype(F32)

    def arrived_in(t, c, h, msg, count, sem):
        items = rs[c].at[t % 2, h, pl.ds(msg, count)]
        remote(items, items, rs_send.at[c, h], rs_recv.at[t % 2, c, h, sem], sib).wait_recv()
        return sum(rs[c][t % 2, h, msg + i].astype(F32) for i in range(count))

    def rs_multiply(t, c):
        @pl.loop(0, 2)
        def _(kk):
            for k in (2 * kk, 2 * kk + 1):
                for h in (0, 1):
                    product(t, c, h, 2, k)
            for k in (0, 1):
                for h in (0, 1):
                    rcopy(t, c, h, part[c].at[h, 2, 2 * kk + k], 2 * kk + k, 2 * kk + k, along(h, True, 1 + 2 * k)).start()

        @pl.loop(0, 2)
        def _(kk):
            for k in (0, 1):
                for h in (0, 1):
                    product(t, c, h, 3 - 2 * k, 2 * kk + k)
            for k in (0, 1):
                for h in (0, 1):
                    po = 3 - 2 * k
                    k2 = 2 * kk + k
                    rcopy(t, c, h, part[c].at[h, po, k2], 5 + 2 * k2 - k, 4 + k2, along(h, True, po)).start()

        @pl.loop(0, 2)
        def _(kk):
            for k in (0, 1):
                for h in (0, 1):
                    product(t, c, h, 1 + 2 * k, 2 * kk + k)

        @pl.loop(0, 2)
        def _(kk):
            for k in (0, 1):
                for h in (0, 1):
                    product(t, c, h, 0, 2 * kk + k)

    def rs_merge(t, c):
        @pl.loop(0, 2)
        def _(kk):
            for k in (0, 1):
                for h in (0, 1):
                    po = 1 + 2 * k
                    k2 = 2 * kk + k
                    got = arrived(t, c, h, k2)
                    part[c][h, po, k2] = (part[c][h, po, k2].astype(F32) + got).astype(BF16)
                    rcopy(t, c, h, part[c].at[h, po, k2], 4 + 2 * k2 + k, 4 + k2, along(h, True, po)).start()

    def summed(t, c, h, k):
        return part[c][h, 0, k].astype(F32) + arrived_in(t, c, h, 4 + 2 * k, 2, 4 + k)

    def rs_second(t, c):
        for k, msg, off in ((0, 12, 2), (1, 13, 1), (3, 14, 3)):
            for h in (0, 1):
                part[c][h, 0, k] = summed(t, c, h, k).astype(BF16)
                rcopy(t, c, h, part[c].at[h, 0, k], msg, 8, along(h, False, off)).start()

    def rs_final(t, c, h):
        carried = summed(t, c, h, 2) + arrived_in(t, c, h, 12, 3, 8)
        return em[t - 1, h, ROWS[c]].astype(F32) * carried

    def rs_sent(t, c):
        for h in (0, 1):
            every = rs[c].at[t % 2, h]
            remote(every, every, rs_send.at[c, h], rs_recv.at[t % 2, c, h, 0], sib).wait_send()

    def keep(t, c, h, weighted):
        states_of(t, c)[row * 2 + h] = weighted.astype(BF16)
        ag_start(t, c, h)

    def finish(t, c):
        if t < STEPS:
            ag_sent(t - 1, c)
        for h in (0, 1):
            weighted = rs_final(t, c, h)
            if t == STEPS:
                wfin[ROWS[c], h * BLOCK : (h + 1) * BLOCK] = weighted
            else:
                keep(t, c, h, weighted)

    def begin(t, c):
        ag_end(t - 1, c)
        if t > 1:
            rs_sent(t - 1, c)
        rs_multiply(t, c)

    def store_emitted(t, c):
        for h in (0, 1):
            em[t - 1, h, ROWS[c]] = e_final(t, c, h).astype(BF16)

    for h in (0, 1):
        e_middle(0, h)
        e_second(0, 0, h)
    for h in (0, 1):
        e_second(0, 1, h)
    for po in (2, 1, 3):
        e_first(1, po)
    for c in (0, 1):
        for h in (0, 1):
            keep(0, c, h, e_final(0, c, h))
    for c in (0, 1):
        ag_relay(0, c, (0, 1, 2))
    blocks_copy().wait()

    def emission(t, part):
        if t > STEPS:
            return
        if part < 3:
            e_first(t, (2, 1, 3)[part])
        elif part < 5:
            if part == 3:
                e_sent2()
            e_middle(t, part - 3)
            e_second(t, 0, part - 3)
        else:
            for h in (0, 1):
                e_second(t, 1, h)

    for t in range(1, STEPS + 1):
        begin(t, 0)
        emission(t, 3)
        emission(t, 4)
        if t > 1:
            finish(t - 1, 1)
        rs_merge(t, 0)
        emission(t, 5)
        if t > 1:
            ag_relay(t - 1, 1, (0, 1, 2))
        rs_second(t, 0)
        begin(t, 1)
        store_emitted(t, 0)
        finish(t, 0)
        emission(t + 1, 0)
        emission(t + 1, 1)
        rs_merge(t, 1)
        emission(t + 1, 2)
        if t < STEPS:
            ag_relay(t, 0, (0, 1, 2))
        rs_second(t, 1)
        store_emitted(t, 1)
    finish(STEPS, 1)

    wide = iota((SEQS, 128), 0) == iota((SEQS, 128), 1)
    total = jnp.sum(wfin[:, :BLOCK] + wfin[:, BLOCK:], axis=1, keepdims=True)
    mine = jnp.sum(jnp.where(wide, total, 0.0), axis=0, keepdims=True)
    ar0[0] = jnp.broadcast_to(mine, (8, 128))
    ar1[row] = ar0[0]

    def a1(i):
        return remote(ar0.at[0], ar1.at[row], a_send.at[0], a_recv.at[0], row_peers[i - 1])

    def a2(i):
        return remote(ar0.at[1], ar2.at[col], a_send.at[1], a_recv.at[1], col_peers[i - 1])

    seven = remote(ar1.at[0:7], ar1.at[0:7], a_send.at[0], a_recv.at[0], sib)
    fifteen = remote(ar2.at[0:15], ar2.at[0:15], a_send.at[1], a_recv.at[1], sib)
    for i in range(1, 8):
        a1(i).start()
    seven.wait_recv()
    ar0[1] = jnp.sum(ar1[...], axis=0)
    ar2[col] = ar0[1]
    for i in range(1, 16):
        a2(i).start()
    fifteen.wait_recv()
    scale_ref[...] = jnp.sum(ar2[...], axis=0) * (1.0 / STATES)

    for c in (0, 1):
        rs_sent(STEPS, c)
        ag_sent(STEPS - 1, c)
    e_sent2()
    for t in range(STEPS + 1):
        remote(pack.at[t], pack.at[t], e_send.at[t], e_recv.at[t, 0], sib).wait_send()
    seven.wait_send()
    fifteen.wait_send()


def normalize(weights_ref, scale_ref, post_ref, log_ref):
    wide = iota((SEQS, 128), 0) == iota((SEQS, 128), 1)
    scale = scale_ref[0:1, :]
    log_ref[...] = jnp.log(scale[:, :SEQS])
    scale_col = jnp.sum(jnp.where(wide, scale, 0.0), axis=1, keepdims=True)
    post_ref[...] = (weights_ref[...] / scale_col).astype(BF16)


def on_device(blocks, source_ids, emission, tokens):
    vocab = emission.shape[0]
    dma = pltpu.SemaphoreType.DMA
    vmem = pltpu.VMEM
    weights, scale = pl.pallas_call(
        kernel,
        out_shape=(jax.ShapeDtypeStruct((SEQS, 2 * BLOCK), F32), jax.ShapeDtypeStruct((8, 128), F32)),
        in_specs=[
            pl.BlockSpec(memory_space=pltpu.SMEM),
            pl.BlockSpec(memory_space=pltpu.VMEM),
            pl.BlockSpec(memory_space=pl.ANY),
            pl.BlockSpec(memory_space=pl.ANY),
        ],
        out_specs=(pl.BlockSpec(memory_space=pltpu.VMEM), pl.BlockSpec(memory_space=pltpu.VMEM)),
        scratch_shapes=[
            vmem((32, BLOCK, BLOCK), BF16),
            vmem((32, vocab, BLOCK), BF16),
            vmem((4 * SLOT, vocab), BF16),
            vmem((STEPS + 1, 2, 3, 4, SLOT, BLOCK), BF16),
            vmem((STEPS + 1, 2, 4, 4, SLOT, BLOCK), BF16),
            vmem((STEPS + 1, 2, 3, 48, BLOCK), BF16),
            vmem((STEPS + 1, 2, 3, 56, BLOCK), BF16),
            vmem((2, 3, 48, BLOCK), BF16),
            vmem((2, 3, 56, BLOCK), BF16),
            vmem((2, SEQS, BLOCK), BF16),
            vmem((STEPS, 2, SEQS, BLOCK), BF16),
            vmem((16, 48, BLOCK), BF16),
            vmem((16, 48, BLOCK), BF16),
            vmem((16, 56, BLOCK), BF16),
            vmem((16, 56, BLOCK), BF16),
            vmem((2, 4, 4, 48, BLOCK), BF16),
            vmem((2, 4, 4, 56, BLOCK), BF16),
            vmem((2, 2, 15, 48, BLOCK), BF16),
            vmem((2, 2, 15, 56, BLOCK), BF16),
            vmem((2, 8, 128), F32),
            vmem((8, 8, 128), F32),
            vmem((16, 8, 128), F32),
            dma,
            dma((32,)),
            dma((STEPS + 1,)),
            dma((STEPS + 1, 2)),
            dma((2,)),
            dma((STEPS + 1, 2, 2)),
            dma((2, 2)),
            dma((2, 2, 2, 4)),
            dma((2, 2)),
            dma((2, 2, 2, 9)),
            dma((2,)),
            dma((2,)),
        ],
        compiler_params=pltpu.CompilerParams(
            collective_id=0, has_side_effects=True, vmem_limit_bytes=63 * 2**20
        ),
        name="forward",
    )(source_ids.reshape(-1), tokens, blocks.reshape(32, BLOCK, BLOCK), emission)
    posterior, logs = pl.pallas_call(
        normalize,
        out_shape=(jax.ShapeDtypeStruct((SEQS, 2 * BLOCK), BF16), jax.ShapeDtypeStruct((1, SEQS), F32)),
        in_specs=[pl.BlockSpec(memory_space=pltpu.VMEM)] * 2,
        out_specs=(pl.BlockSpec(memory_space=pltpu.VMEM), pl.BlockSpec(memory_space=pltpu.VMEM)),
        name="normalize",
    )(weights, scale)
    return posterior, logs.reshape(SEQS)


def solution(mesh):
    in_specs = (P("row", "col", None, None), P("row", "col"), P("col", "row"), P())
    out_specs = (P(None, ("row", "col")), P())
    return jax.shard_map(on_device, mesh=mesh, in_specs=in_specs, out_specs=out_specs, check_vma=False)
```

```python
import functools

import jax
import jax.numpy as jnp
from jax import lax
from jax.experimental import pallas as pl
from jax.experimental.pallas import tpu as pltpu
from jax.sharding import PartitionSpec as P

MESH = pl.DeviceIdType.MESH
STATES = 131072
SEQS = 104
CAP = 26
SLOT = 32
BLOCK = 512
STEPS = 3
ROWS = (slice(0, 48), slice(48, 104))
QOFF = (2, 1, 3, 0)
F32 = jnp.float32
BF16 = jnp.bfloat16


def iota(shape, dim):
    return lax.broadcasted_iota(jnp.int32, shape, dim).astype(F32)


def kernel(
    ids_ref, tok_ref, blocks_hbm, emis_hbm, wfin, scale_ref,
    blocks_v, emis_v, sel_v, pack, land1, land2_a, land2_b, mid_a, mid_b, own, em, states_a, states_b, states_c, states_d, part_a, part_b, rs_a, rs_b, ar0, ar1, ar2,
    blk_sem, emis_sem, e_send, e_recv, e_send2, e_recv2, ag_send, ag_recv, rs_send, rs_recv, a_send, a_recv,
):
    row = lax.axis_index("row")
    col = lax.axis_index("col")
    y, core = row // 2, row % 2
    x, z = col // 4, col % 4
    vocab = emis_v.shape[1]
    states = (states_a, states_b, states_c, states_d)
    land2 = (land2_a, land2_b)
    mid = (mid_a, mid_b)
    part = (part_a, part_b)
    rs = (rs_a, rs_b)

    def at_plane(xd, zd):
        return (row, (xd % 4) * 4 + zd % 4)

    def along(h, first, off):
        if (h == 0) == first:
            return at_plane(x + off, z)
        return at_plane(x, z + off)

    def pq(h):
        return (x, z) if h == 0 else (z, x)

    def at_y(off):
        return (((y + off) % 4) * 2 + core, col)

    sib = (row + 1 - 2 * core, col)

    def remote(src, dst, ssem, rsem, dev):
        return pltpu.make_async_remote_copy(
            src_ref=src, dst_ref=dst, send_sem=ssem, recv_sem=rsem, device_id=dev, device_id_type=MESH
        )

    def emis_copy(chunk):
        return pltpu.make_async_copy(
            emis_hbm.at[:, pl.ds(pl.multiple_of(chunk * BLOCK, BLOCK), BLOCK)], emis_v.at[chunk], emis_sem.at[chunk]
        )

    def chunk_of(h, po, qd):
        p, _ = pq(h)
        pd = (p + po) % 4
        return (pd * 4 + qd) * 2 if h == 0 else (qd * 4 + pd) * 2 + 1

    groups = [(half, po) for half in (0, 1) for po in (2, 1, 3)] + [(0, 0), (1, 0)]

    def chunks(half, po, h):
        _, q = pq(h)
        return [(i, chunk_of(h, po, (q + QOFF[i]) % 4)) for i in (2 * half, 2 * half + 1)]

    for half, po in groups:
        for h in (0, 1):
            for _, chunk in chunks(half, po, h):
                emis_copy(chunk).start()

    def blocks_copy():
        return pltpu.make_async_copy(blocks_hbm, blocks_v, blk_sem)

    blocks_copy().start()

    barrier = pltpu.get_barrier_semaphore()
    row_peers = [(lax.rem(row + i, 8), col) for i in range(1, 8)]
    col_peers = [(row, lax.rem(col + i, 16)) for i in range(1, 16)]
    for dev in row_peers + col_peers:
        pl.semaphore_signal(barrier, inc=1, device_id=dev, device_id_type=MESH)

    eye = iota((SEQS, SEQS), 0) == iota((SEQS, SEQS), 1)
    before = iota((SEQS, SEQS), 0) < iota((SEQS, SEQS), 1)

    def to_col(v):
        return jnp.sum(jnp.where(eye, v, 0.0), axis=1, keepdims=True)

    def places(t):
        tok_row = tok_ref[t : t + 1, :].astype(F32)
        owner_row = jnp.zeros_like(tok_row)
        for k in range(1, 16):
            owner_row += jnp.where(tok_row >= float(k * vocab), 1.0, 0.0)
        owner_col = to_col(owner_row)
        same = jnp.where((owner_col == owner_row) & before, 1.0, 0.0)
        pos_row = jnp.sum(same, axis=0, keepdims=True)
        return tok_row, owner_row, owner_col, pos_row

    for t in range(STEPS + 1):
        tok_row, owner_row, owner_col, pos_row = places(t)
        me = col.astype(F32)
        slot_of = jnp.where((pos_row == iota((SLOT, SEQS), 0)) & (owner_row == me), 1.0, 0.0).astype(BF16)
        id_of = jnp.where(to_col(tok_row) - me * float(vocab) == iota((SEQS, vocab), 1), 1.0, 0.0).astype(BF16)
        sel_v[t * SLOT : (t + 1) * SLOT, :] = jnp.dot(slot_of, id_of, preferred_element_type=F32).astype(BF16)

    def e1(t, h, po, part=slice(0, 4)):
        p, _ = pq(h)
        return remote(
            pack.at[t, h, po - 1, part], land1.at[t, h, part, p], e_send.at[t], e_recv.at[t, h, part.start // 2],
            along(h, True, po),
        )

    def e1_arrived(t, h, part=slice(0, 4)):
        three = land1.at[t, h, part, 0:3]
        remote(three, three, e_send.at[t], e_recv.at[t, h, part.start // 2], sib).wait_recv()

    def e2(t, c, h, qo):
        return remote(
            mid[c].at[h, qo - 1], land2[c].at[t, h, qo - 1], e_send2.at[c], e_recv2.at[t, c, h], along(h, False, qo)
        )

    for half, po in groups:
        for h in (0, 1):
            p, _ = pq(h)
            for i, chunk in chunks(half, po, h):
                emis_copy(chunk).wait()
                rows = jnp.dot(sel_v[...], emis_v[chunk], preferred_element_type=F32).astype(BF16)
                for t in range(STEPS + 1):
                    piece = rows[t * SLOT : (t + 1) * SLOT]
                    if po:
                        pack[t, h, po - 1, i] = piece
                    else:
                        land1[t, h, i, p] = piece
            if (half, po, h) == (0, 2, 0):
                pl.semaphore_wait(barrier, 22)
            if po:
                e1(0, h, po, slice(2 * half, 2 * half + 2)).start()

    def e_first(t, po):
        for h in (0, 1):
            e1(t, h, po).start()

    def e_sent2():
        for c in (0, 1):
            remote(mid[c], mid[c], e_send2.at[c], e_recv2.at[0, c, 0], sib).wait_send()

    def e_pick(t, h):
        _, q = pq(h)
        _, _, owner_col, pos_row = places(t)
        x_of = jnp.zeros_like(owner_col)
        for k in range(1, 4):
            x_of += jnp.where(owner_col >= float(4 * k), 1.0, 0.0)
        z_of = owner_col - 4.0 * x_of
        p_of, q_of = (x_of, z_of) if h == 0 else (z_of, x_of)
        place = p_of * float(SLOT) + to_col(pos_row)
        lane = iota((SEQS, 4 * SLOT), 1)
        return jnp.where((lane == place) & (q_of == q.astype(F32)), 1.0, 0.0).astype(BF16)

    def e_place(t, h, pick, i):
        rows = jnp.dot(pick, land1[t, h, i].reshape(4 * SLOT, BLOCK), preferred_element_type=F32).astype(BF16)
        if QOFF[i]:
            for c in (0, 1):
                mid[c][h, QOFF[i] - 1] = rows[ROWS[c]]
        else:
            own[h] = rows

    def e_middle(t, h):
        pick = e_pick(t, h)
        e1_arrived(t, h)
        for i in range(4):
            e_place(t, h, pick, i)

    def e_second(t, c, h):
        for qo in (2, 1, 3):
            e2(t, c, h, qo).start()

    def e_final(t, c, h):
        three = land2[c].at[t, h]
        remote(three, three, e_send2.at[c], e_recv2.at[t, c, h], sib).wait_recv()
        return own[h, ROWS[c]].astype(F32) + sum(land2[c][t, h, i].astype(F32) for i in range(3))

    def states_of(t, c):
        return states[c * 2 + t % 2]

    def ag(t, c, h, of_row, sem, dev):
        item = states_of(t, c).at[of_row * 2 + h]
        return remote(item, item, ag_send.at[c, h], ag_recv.at[t % 2, c, h, sem], dev)

    def same_core(off):
        return ((y + off) % 4) * 2 + core

    def ag_start(t, c, h):
        for sem, off in enumerate((1, 3, 2)):
            ag(t, c, h, row, sem, at_y(off)).start()
        ag(t, c, h, row, 3, sib).start()

    def ag_relay(t, c, sems):
        for sem in sems:
            for h in (0, 1):
                of = same_core((3, 1, 2)[sem])
                ag(t, c, h, of, sem, sib).wait_recv()
                ag(t, c, h, of, 3, sib).start()

    def ag_end(t, c):
        for h in (0, 1):
            four = states_of(t, c).at[0:4]
            remote(four, four, ag_send.at[c, h], ag_recv.at[t % 2, c, h, 3], sib).wait_recv()

    def ag_sent(t, c):
        for h in (0, 1):
            seven = states_of(t, c).at[0:7]
            remote(seven, seven, ag_send.at[c, h], ag_recv.at[t % 2, c, h, 3], sib).wait_send()

    def product(t, c, h, po, k):
        p, q = pq(h)
        pd = (p + po) % 4
        qd = (q + 2 - k + 4) % 4
        dest = (pd * 4 + qd) * 2 if h == 0 else (qd * 4 + pd) * 2 + 1
        sid = ids_ref[dest]
        local = (sid // 32) * 2 + sid % 2
        acc = jnp.dot(states_of(t - 1, c)[local], blocks_v[dest], preferred_element_type=F32)
        part[c][h, po, k] = acc.astype(BF16)

    def rcopy(t, c, h, src, msg, sem, dev):
        return remote(src, rs[c].at[t % 2, h, msg], rs_send.at[c, h], rs_recv.at[t % 2, c, h, sem], dev)

    def arrived(t, c, h, k):
        rcopy(t, c, h, rs[c].at[t % 2, h, k], k, k, sib).wait_recv()
        return rs[c][t % 2, h, k].astype(F32)

    def arrived_in(t, c, h, msg, count, sem):
        items = rs[c].at[t % 2, h, pl.ds(msg, count)]
        remote(items, items, rs_send.at[c, h], rs_recv.at[t % 2, c, h, sem], sib).wait_recv()
        return sum(rs[c][t % 2, h, msg + i].astype(F32) for i in range(count))

    def rs_multiply(t, c):
        @pl.loop(0, 2)
        def _(kk):
            for k in (2 * kk, 2 * kk + 1):
                for h in (0, 1):
                    product(t, c, h, 2, k)
            for k in (0, 1):
                for h in (0, 1):
                    rcopy(t, c, h, part[c].at[h, 2, 2 * kk + k], 2 * kk + k, 2 * kk + k, along(h, True, 1 + 2 * k)).start()

        @pl.loop(0, 2)
        def _(kk):
            for k in (0, 1):
                for h in (0, 1):
                    product(t, c, h, 3 - 2 * k, 2 * kk + k)
            for k in (0, 1):
                for h in (0, 1):
                    po = 3 - 2 * k
                    k2 = 2 * kk + k
                    rcopy(t, c, h, part[c].at[h, po, k2], 5 + 2 * k2 - k, 4 + k2, along(h, True, po)).start()

        @pl.loop(0, 2)
        def _(kk):
            for k in (0, 1):
                for h in (0, 1):
                    product(t, c, h, 1 + 2 * k, 2 * kk + k)

        @pl.loop(0, 2)
        def _(kk):
            for k in (0, 1):
                for h in (0, 1):
                    product(t, c, h, 0, 2 * kk + k)

    def rs_merge(t, c):
        @pl.loop(0, 2)
        def _(kk):
            for k in (0, 1):
                for h in (0, 1):
                    po = 1 + 2 * k
                    k2 = 2 * kk + k
                    got = arrived(t, c, h, k2)
                    part[c][h, po, k2] = (part[c][h, po, k2].astype(F32) + got).astype(BF16)
                    rcopy(t, c, h, part[c].at[h, po, k2], 4 + 2 * k2 + k, 4 + k2, along(h, True, po)).start()

    def summed(t, c, h, k):
        return part[c][h, 0, k].astype(F32) + arrived_in(t, c, h, 4 + 2 * k, 2, 4 + k)

    def rs_second(t, c):
        for k, msg, off in ((0, 12, 2), (1, 13, 1), (3, 14, 3)):
            for h in (0, 1):
                part[c][h, 0, k] = summed(t, c, h, k).astype(BF16)
                rcopy(t, c, h, part[c].at[h, 0, k], msg, 8, along(h, False, off)).start()

    def rs_final(t, c, h):
        carried = summed(t, c, h, 2) + arrived_in(t, c, h, 12, 3, 8)
        return em[t - 1, h, ROWS[c]].astype(F32) * carried

    def rs_sent(t, c):
        for h in (0, 1):
            every = rs[c].at[t % 2, h]
            remote(every, every, rs_send.at[c, h], rs_recv.at[t % 2, c, h, 0], sib).wait_send()

    def keep(t, c, h, weighted):
        states_of(t, c)[row * 2 + h] = weighted.astype(BF16)
        ag_start(t, c, h)

    def finish(t, c):
        if t < STEPS:
            ag_sent(t - 1, c)
        for h in (0, 1):
            weighted = rs_final(t, c, h)
            if t == STEPS:
                wfin[ROWS[c], h * BLOCK : (h + 1) * BLOCK] = weighted
            else:
                keep(t, c, h, weighted)

    def begin(t, c):
        ag_end(t - 1, c)
        if t > 1:
            rs_sent(t - 1, c)
        rs_multiply(t, c)

    def store_emitted(t, c):
        for h in (0, 1):
            em[t - 1, h, ROWS[c]] = e_final(t, c, h).astype(BF16)

    picks = [e_pick(0, h) for h in (0, 1)]
    for half in (0, 1):
        for h in (0, 1):
            e1_arrived(0, h, slice(2 * half, 2 * half + 2))
            for i in (2 * half, 2 * half + 1):
                e_place(0, h, picks[h], i)
                if QOFF[i]:
                    e2(0, 0, h, QOFF[i]).start()
        for h in (0, 1):
            for i in (2 * half, 2 * half + 1):
                if QOFF[i]:
                    e2(0, 1, h, QOFF[i]).start()
    for po in (2, 1, 3):
        e_first(1, po)
    for c in (0, 1):
        for h in (0, 1):
            keep(0, c, h, e_final(0, c, h))
    for c in (0, 1):
        ag_relay(0, c, (0, 1, 2))
    blocks_copy().wait()

    def emission(t, part):
        if t > STEPS:
            return
        if part < 3:
            e_first(t, (2, 1, 3)[part])
        elif part < 5:
            if part == 3:
                e_sent2()
            e_middle(t, part - 3)
            e_second(t, 0, part - 3)
        else:
            for h in (0, 1):
                e_second(t, 1, h)

    for t in range(1, STEPS + 1):
        begin(t, 0)
        emission(t, 3)
        if t > 1:
            finish(t - 1, 1)
        rs_merge(t, 0)
        emission(t, 4)
        emission(t, 5)
        if t > 1:
            ag_relay(t - 1, 1, (0, 1, 2))
        rs_second(t, 0)
        begin(t, 1)
        store_emitted(t, 0)
        finish(t, 0)
        emission(t + 1, 0)
        rs_merge(t, 1)
        emission(t + 1, 1)
        emission(t + 1, 2)
        if t < STEPS:
            ag_relay(t, 0, (0, 1, 2))
        rs_second(t, 1)
        store_emitted(t, 1)
    finish(STEPS, 1)

    wide = iota((SEQS, 128), 0) == iota((SEQS, 128), 1)
    total = jnp.sum(wfin[:, :BLOCK] + wfin[:, BLOCK:], axis=1, keepdims=True)
    mine = jnp.sum(jnp.where(wide, total, 0.0), axis=0, keepdims=True)
    ar0[0] = jnp.broadcast_to(mine, (8, 128))
    ar1[row] = ar0[0]

    def a1(i):
        return remote(ar0.at[0], ar1.at[row], a_send.at[0], a_recv.at[0], row_peers[i - 1])

    def a2(i):
        return remote(ar0.at[1], ar2.at[col], a_send.at[1], a_recv.at[1], col_peers[i - 1])

    seven = remote(ar1.at[0:7], ar1.at[0:7], a_send.at[0], a_recv.at[0], sib)
    fifteen = remote(ar2.at[0:15], ar2.at[0:15], a_send.at[1], a_recv.at[1], sib)
    for i in range(1, 8):
        a1(i).start()
    seven.wait_recv()
    ar0[1] = jnp.sum(ar1[...], axis=0)
    ar2[col] = ar0[1]
    for i in range(1, 16):
        a2(i).start()
    fifteen.wait_recv()
    scale_ref[...] = jnp.sum(ar2[...], axis=0) * (1.0 / STATES)

    for c in (0, 1):
        rs_sent(STEPS, c)
        ag_sent(STEPS - 1, c)
    e_sent2()
    for t in range(STEPS + 1):
        remote(pack.at[t], pack.at[t], e_send.at[t], e_recv.at[t, 0], sib).wait_send()
    seven.wait_send()
    fifteen.wait_send()


def normalize(weights_ref, scale_ref, post_ref, log_ref):
    wide = iota((SEQS, 128), 0) == iota((SEQS, 128), 1)
    scale = scale_ref[0:1, :]
    log_ref[...] = jnp.log(scale[:, :SEQS])
    scale_col = jnp.sum(jnp.where(wide, scale, 0.0), axis=1, keepdims=True)
    post_ref[...] = (weights_ref[...] / scale_col).astype(BF16)


def on_device(blocks, source_ids, emission, tokens):
    vocab = emission.shape[0]
    dma = pltpu.SemaphoreType.DMA
    vmem = pltpu.VMEM
    weights, scale = pl.pallas_call(
        kernel,
        out_shape=(jax.ShapeDtypeStruct((SEQS, 2 * BLOCK), F32), jax.ShapeDtypeStruct((8, 128), F32)),
        in_specs=[
            pl.BlockSpec(memory_space=pltpu.SMEM),
            pl.BlockSpec(memory_space=pltpu.VMEM),
            pl.BlockSpec(memory_space=pl.ANY),
            pl.BlockSpec(memory_space=pl.ANY),
        ],
        out_specs=(pl.BlockSpec(memory_space=pltpu.VMEM), pl.BlockSpec(memory_space=pltpu.VMEM)),
        scratch_shapes=[
            vmem((32, BLOCK, BLOCK), BF16),
            vmem((32, vocab, BLOCK), BF16),
            vmem((4 * SLOT, vocab), BF16),
            vmem((STEPS + 1, 2, 3, 4, SLOT, BLOCK), BF16),
            vmem((STEPS + 1, 2, 4, 4, SLOT, BLOCK), BF16),
            vmem((STEPS + 1, 2, 3, 48, BLOCK), BF16),
            vmem((STEPS + 1, 2, 3, 56, BLOCK), BF16),
            vmem((2, 3, 48, BLOCK), BF16),
            vmem((2, 3, 56, BLOCK), BF16),
            vmem((2, SEQS, BLOCK), BF16),
            vmem((STEPS, 2, SEQS, BLOCK), BF16),
            vmem((16, 48, BLOCK), BF16),
            vmem((16, 48, BLOCK), BF16),
            vmem((16, 56, BLOCK), BF16),
            vmem((16, 56, BLOCK), BF16),
            vmem((2, 4, 4, 48, BLOCK), BF16),
            vmem((2, 4, 4, 56, BLOCK), BF16),
            vmem((2, 2, 15, 48, BLOCK), BF16),
            vmem((2, 2, 15, 56, BLOCK), BF16),
            vmem((2, 8, 128), F32),
            vmem((8, 8, 128), F32),
            vmem((16, 8, 128), F32),
            dma,
            dma((32,)),
            dma((STEPS + 1,)),
            dma((STEPS + 1, 2, 2)),
            dma((2,)),
            dma((STEPS + 1, 2, 2)),
            dma((2, 2)),
            dma((2, 2, 2, 4)),
            dma((2, 2)),
            dma((2, 2, 2, 9)),
            dma((2,)),
            dma((2,)),
        ],
        compiler_params=pltpu.CompilerParams(
            collective_id=0, has_side_effects=True, vmem_limit_bytes=63 * 2**20
        ),
        name="forward",
    )(source_ids.reshape(-1), tokens, blocks.reshape(32, BLOCK, BLOCK), emission)
    posterior, logs = pl.pallas_call(
        normalize,
        out_shape=(jax.ShapeDtypeStruct((SEQS, 2 * BLOCK), BF16), jax.ShapeDtypeStruct((1, SEQS), F32)),
        in_specs=[pl.BlockSpec(memory_space=pltpu.VMEM)] * 2,
        out_specs=(pl.BlockSpec(memory_space=pltpu.VMEM), pl.BlockSpec(memory_space=pltpu.VMEM)),
        name="normalize",
    )(weights, scale)
    return posterior, logs.reshape(SEQS)


def solution(mesh):
    in_specs = (P("row", "col", None, None), P("row", "col"), P("col", "row"), P())
    out_specs = (P(None, ("row", "col")), P())
    return jax.shard_map(on_device, mesh=mesh, in_specs=in_specs, out_specs=out_specs, check_vma=False)
```

```python
import functools

import jax
import jax.numpy as jnp
from jax import lax
from jax.experimental import pallas as pl
from jax.experimental.pallas import tpu as pltpu
from jax.sharding import PartitionSpec as P

MESH = pl.DeviceIdType.MESH
STATES = 131072
SEQS = 104
CAP = 26
SLOT = 32
TIGHT = 80
BLOCK = 512
STEPS = 3
ROWS = (slice(0, 48), slice(48, 104))
QOFF = (2, 1, 3, 0)
F32 = jnp.float32
BF16 = jnp.bfloat16


def iota(shape, dim):
    return lax.broadcasted_iota(jnp.int32, shape, dim).astype(F32)


def kernel(
    ids_ref, tok_ref, blocks_hbm, emis_hbm, wfin, scale_ref,
    blocks_v, emis_v, sel_v, pack, pack_c, land1, land1_c, land2_a, land2_b, mid_a, mid_b, own, em, states_a, states_b, states_c, states_d, part_a, part_b, rs_a, rs_b, ar0, ar1, ar2,
    blk_sem, emis_sem, e_send, e_recv, e_send2, e_recv2, ag_send, ag_recv, rs_send, rs_recv, a_send, a_recv,
):
    row = lax.axis_index("row")
    col = lax.axis_index("col")
    y, core = row // 2, row % 2
    x, z = col // 4, col % 4
    vocab = emis_v.shape[1]
    states = (states_a, states_b, states_c, states_d)
    packs = [pack.at[t] for t in range(STEPS)] + [pack_c]
    lands = [land1.at[t] for t in range(STEPS)] + [land1_c]
    land2 = (land2_a, land2_b)
    mid = (mid_a, mid_b)
    part = (part_a, part_b)
    rs = (rs_a, rs_b)

    def at_plane(xd, zd):
        return (row, (xd % 4) * 4 + zd % 4)

    def along(h, first, off):
        if (h == 0) == first:
            return at_plane(x + off, z)
        return at_plane(x, z + off)

    def pq(h):
        return (x, z) if h == 0 else (z, x)

    def at_y(off):
        return (((y + off) % 4) * 2 + core, col)

    sib = (row + 1 - 2 * core, col)

    def remote(src, dst, ssem, rsem, dev):
        return pltpu.make_async_remote_copy(
            src_ref=src, dst_ref=dst, send_sem=ssem, recv_sem=rsem, device_id=dev, device_id_type=MESH
        )

    def emis_copy(chunk):
        return pltpu.make_async_copy(
            emis_hbm.at[:, pl.ds(pl.multiple_of(chunk * BLOCK, BLOCK), BLOCK)], emis_v.at[chunk], emis_sem.at[chunk]
        )

    def chunk_of(h, po, qd):
        p, _ = pq(h)
        pd = (p + po) % 4
        return (pd * 4 + qd) * 2 if h == 0 else (qd * 4 + pd) * 2 + 1

    groups = [(half, po) for half in (0, 1) for po in (2, 1, 3)] + [(0, 0), (1, 0)]

    def chunks(half, po, h):
        _, q = pq(h)
        return [(i, chunk_of(h, po, (q + QOFF[i]) % 4)) for i in (2 * half, 2 * half + 1)]

    for half, po in groups:
        for h in (0, 1):
            for _, chunk in chunks(half, po, h):
                emis_copy(chunk).start()

    def blocks_copy():
        return pltpu.make_async_copy(blocks_hbm, blocks_v, blk_sem)

    blocks_copy().start()

    barrier = pltpu.get_barrier_semaphore()
    row_peers = [(lax.rem(row + i, 8), col) for i in range(1, 8)]
    col_peers = [(row, lax.rem(col + i, 16)) for i in range(1, 16)]
    for dev in row_peers + col_peers:
        pl.semaphore_signal(barrier, inc=1, device_id=dev, device_id_type=MESH)

    eye = iota((SEQS, SEQS), 0) == iota((SEQS, SEQS), 1)
    before = iota((SEQS, SEQS), 0) < iota((SEQS, SEQS), 1)

    def to_col(v):
        return jnp.sum(jnp.where(eye, v, 0.0), axis=1, keepdims=True)

    def places(t):
        tok_row = tok_ref[t : t + 1, :].astype(F32)
        owner_row = jnp.zeros_like(tok_row)
        for k in range(1, 16):
            owner_row += jnp.where(tok_row >= float(k * vocab), 1.0, 0.0)
        owner_col = to_col(owner_row)
        same = jnp.where((owner_col == owner_row) & before, 1.0, 0.0)
        pos_row = jnp.sum(same, axis=0, keepdims=True)
        return tok_row, owner_row, owner_col, pos_row

    me = col.astype(F32)

    def chosen(t, rows, start):
        tok_row, owner_row, _, pos_row = places(t)
        slot_of = jnp.where((pos_row + float(start) == iota((rows, SEQS), 0)) & (owner_row == me), 1.0, 0.0).astype(BF16)
        id_of = jnp.where(to_col(tok_row) - me * float(vocab) == iota((SEQS, vocab), 1), 1.0, 0.0).astype(BF16)
        return jnp.dot(slot_of, id_of, preferred_element_type=F32)

    sel_v[:SLOT, :] = chosen(0, SLOT, 0).astype(BF16)
    sel_v[SLOT:, :] = sum(chosen(t, TIGHT, CAP * (t - 1)) for t in range(1, STEPS + 1)).astype(BF16)

    def e1(t, h, po, part=slice(0, 4)):
        p, _ = pq(h)
        return remote(
            packs[t].at[h, po - 1, part], lands[t].at[h, part, p], e_send.at[t], e_recv.at[t, h, part.start // 2],
            along(h, True, po),
        )

    def e1_arrived(t, h, part=slice(0, 4)):
        three = lands[t].at[h, part, 0:3]
        remote(three, three, e_send.at[t], e_recv.at[t, h, part.start // 2], sib).wait_recv()

    def e2(t, c, h, qo):
        return remote(
            mid[c].at[h, qo - 1], land2[c].at[t, h, qo - 1], e_send2.at[c], e_recv2.at[t, c, h], along(h, False, qo)
        )

    for half, po in groups:
        for h in (0, 1):
            p, _ = pq(h)
            for i, chunk in chunks(half, po, h):
                emis_copy(chunk).wait()
                rows = jnp.dot(sel_v[...], emis_v[chunk], preferred_element_type=F32).astype(BF16)
                for t in range(STEPS + 1):
                    piece = rows[t * SLOT : min((t + 1) * SLOT, SLOT + TIGHT)]
                    if po:
                        packs[t][h, po - 1, i] = piece
                    else:
                        lands[t][h, i, p] = piece
            if (half, po, h) == (0, 2, 0):
                pl.semaphore_wait(barrier, 22)
            if po:
                e1(0, h, po, slice(2 * half, 2 * half + 2)).start()

    def e_first(t, po):
        for h in (0, 1):
            e1(t, h, po).start()

    def e_sent2():
        for c in (0, 1):
            remote(mid[c], mid[c], e_send2.at[c], e_recv2.at[0, c, 0], sib).wait_send()

    def e_pick(t, h):
        _, q = pq(h)
        _, _, owner_col, pos_row = places(t)
        x_of = jnp.zeros_like(owner_col)
        for k in range(1, 4):
            x_of += jnp.where(owner_col >= float(4 * k), 1.0, 0.0)
        z_of = owner_col - 4.0 * x_of
        p_of, q_of = (x_of, z_of) if h == 0 else (z_of, x_of)
        place = to_col(pos_row) + float(CAP * max(t - 1, 0))
        picks = []
        for n in ((0,), (1,), (1, 2), (2, 3))[t]:
            width = lands[n].shape[3]
            there = place - float(SLOT * max(n - 1, 0))
            mine = (there >= 0.0) & (there < float(width)) & (q_of == q.astype(F32))
            lane = iota((SEQS, 4 * width), 1)
            picks.append((n, jnp.where((lane == p_of * float(width) + there) & mine, 1.0, 0.0).astype(BF16)))
        return picks

    def e_place(t, h, picks, i):
        rows = sum(
            jnp.dot(pick, lands[n][h, i].reshape(-1, BLOCK), preferred_element_type=F32) for n, pick in picks
        ).astype(BF16)
        if QOFF[i]:
            for c in (0, 1):
                mid[c][h, QOFF[i] - 1] = rows[ROWS[c]]
        else:
            own[h] = rows

    def e_middle(t, h):
        pick = e_pick(t, h)
        e1_arrived(t, h)
        for i in range(4):
            e_place(t, h, pick, i)

    def e_second(t, c, h):
        for qo in (2, 1, 3):
            e2(t, c, h, qo).start()

    def e_final(t, c, h):
        three = land2[c].at[t, h]
        remote(three, three, e_send2.at[c], e_recv2.at[t, c, h], sib).wait_recv()
        return own[h, ROWS[c]].astype(F32) + sum(land2[c][t, h, i].astype(F32) for i in range(3))

    def states_of(t, c):
        return states[c * 2 + t % 2]

    def ag(t, c, h, of_row, sem, dev):
        item = states_of(t, c).at[of_row * 2 + h]
        return remote(item, item, ag_send.at[c, h], ag_recv.at[t % 2, c, h, sem], dev)

    def same_core(off):
        return ((y + off) % 4) * 2 + core

    def ag_start(t, c, h):
        for sem, off in enumerate((1, 3, 2)):
            ag(t, c, h, row, sem, at_y(off)).start()
        ag(t, c, h, row, 3, sib).start()

    def ag_relay(t, c, sems):
        for sem in sems:
            for h in (0, 1):
                of = same_core((3, 1, 2)[sem])
                ag(t, c, h, of, sem, sib).wait_recv()
                ag(t, c, h, of, 3, sib).start()

    def ag_end(t, c):
        for h in (0, 1):
            four = states_of(t, c).at[0:4]
            remote(four, four, ag_send.at[c, h], ag_recv.at[t % 2, c, h, 3], sib).wait_recv()

    def ag_sent(t, c):
        for h in (0, 1):
            seven = states_of(t, c).at[0:7]
            remote(seven, seven, ag_send.at[c, h], ag_recv.at[t % 2, c, h, 3], sib).wait_send()

    def product(t, c, h, po, k):
        p, q = pq(h)
        pd = (p + po) % 4
        qd = (q + 2 - k + 4) % 4
        dest = (pd * 4 + qd) * 2 if h == 0 else (qd * 4 + pd) * 2 + 1
        sid = ids_ref[dest]
        local = (sid // 32) * 2 + sid % 2
        acc = jnp.dot(states_of(t - 1, c)[local], blocks_v[dest], preferred_element_type=F32)
        part[c][h, po, k] = acc.astype(BF16)

    def rcopy(t, c, h, src, msg, sem, dev):
        return remote(src, rs[c].at[t % 2, h, msg], rs_send.at[c, h], rs_recv.at[t % 2, c, h, sem], dev)

    def arrived(t, c, h, k):
        rcopy(t, c, h, rs[c].at[t % 2, h, k], k, k, sib).wait_recv()
        return rs[c][t % 2, h, k].astype(F32)

    def arrived_in(t, c, h, msg, count, sem):
        items = rs[c].at[t % 2, h, pl.ds(msg, count)]
        remote(items, items, rs_send.at[c, h], rs_recv.at[t % 2, c, h, sem], sib).wait_recv()
        return sum(rs[c][t % 2, h, msg + i].astype(F32) for i in range(count))

    def rs_multiply(t, c):
        @pl.loop(0, 2)
        def _(kk):
            for k in (2 * kk, 2 * kk + 1):
                for h in (0, 1):
                    product(t, c, h, 2, k)
            for k in (0, 1):
                for h in (0, 1):
                    rcopy(t, c, h, part[c].at[h, 2, 2 * kk + k], 2 * kk + k, 2 * kk + k, along(h, True, 1 + 2 * k)).start()

        @pl.loop(0, 2)
        def _(kk):
            for k in (0, 1):
                for h in (0, 1):
                    product(t, c, h, 3 - 2 * k, 2 * kk + k)
            for k in (0, 1):
                for h in (0, 1):
                    po = 3 - 2 * k
                    k2 = 2 * kk + k
                    rcopy(t, c, h, part[c].at[h, po, k2], 5 + 2 * k2 - k, 4 + k2, along(h, True, po)).start()

        @pl.loop(0, 2)
        def _(kk):
            for k in (0, 1):
                for h in (0, 1):
                    product(t, c, h, 1 + 2 * k, 2 * kk + k)

        @pl.loop(0, 2)
        def _(kk):
            for k in (0, 1):
                for h in (0, 1):
                    product(t, c, h, 0, 2 * kk + k)

    def rs_merge(t, c):
        @pl.loop(0, 2)
        def _(kk):
            for k in (0, 1):
                for h in (0, 1):
                    po = 1 + 2 * k
                    k2 = 2 * kk + k
                    got = arrived(t, c, h, k2)
                    part[c][h, po, k2] = (part[c][h, po, k2].astype(F32) + got).astype(BF16)
                    rcopy(t, c, h, part[c].at[h, po, k2], 4 + 2 * k2 + k, 4 + k2, along(h, True, po)).start()

    def summed(t, c, h, k):
        return part[c][h, 0, k].astype(F32) + arrived_in(t, c, h, 4 + 2 * k, 2, 4 + k)

    def rs_second(t, c):
        for k, msg, off in ((0, 12, 2), (1, 13, 1), (3, 14, 3)):
            for h in (0, 1):
                part[c][h, 0, k] = summed(t, c, h, k).astype(BF16)
                rcopy(t, c, h, part[c].at[h, 0, k], msg, 8, along(h, False, off)).start()

    def rs_final(t, c, h):
        carried = summed(t, c, h, 2) + arrived_in(t, c, h, 12, 3, 8)
        return em[t - 1, h, ROWS[c]].astype(F32) * carried

    def rs_sent(t, c):
        for h in (0, 1):
            every = rs[c].at[t % 2, h]
            remote(every, every, rs_send.at[c, h], rs_recv.at[t % 2, c, h, 0], sib).wait_send()

    def keep(t, c, h, weighted):
        states_of(t, c)[row * 2 + h] = weighted.astype(BF16)
        ag_start(t, c, h)

    def finish(t, c):
        if t < STEPS:
            ag_sent(t - 1, c)
        for h in (0, 1):
            weighted = rs_final(t, c, h)
            if t == STEPS:
                wfin[ROWS[c], h * BLOCK : (h + 1) * BLOCK] = weighted
            else:
                keep(t, c, h, weighted)

    def begin(t, c):
        ag_end(t - 1, c)
        if t > 1:
            rs_sent(t - 1, c)
        rs_multiply(t, c)

    def store_emitted(t, c):
        for h in (0, 1):
            em[t - 1, h, ROWS[c]] = e_final(t, c, h).astype(BF16)

    picks = [e_pick(0, h) for h in (0, 1)]
    for half in (0, 1):
        for h in (0, 1):
            e1_arrived(0, h, slice(2 * half, 2 * half + 2))
            for i in (2 * half, 2 * half + 1):
                e_place(0, h, picks[h], i)
                if QOFF[i]:
                    e2(0, 0, h, QOFF[i]).start()
        for h in (0, 1):
            for i in (2 * half, 2 * half + 1):
                if QOFF[i]:
                    e2(0, 1, h, QOFF[i]).start()
    for po in (2, 1, 3):
        e_first(1, po)
    for c in (0, 1):
        for h in (0, 1):
            keep(0, c, h, e_final(0, c, h))
    for c in (0, 1):
        ag_relay(0, c, (0, 1, 2))
    blocks_copy().wait()

    def emission(t, part):
        if t > STEPS:
            return
        if part < 3:
            e_first(t, (2, 1, 3)[part])
        elif part < 5:
            if part == 3:
                e_sent2()
            e_middle(t, part - 3)
            e_second(t, 0, part - 3)
        else:
            for h in (0, 1):
                e_second(t, 1, h)

    for t in range(1, STEPS + 1):
        begin(t, 0)
        emission(t, 3)
        if t > 1:
            finish(t - 1, 1)
        rs_merge(t, 0)
        emission(t, 4)
        emission(t, 5)
        if t > 1:
            ag_relay(t - 1, 1, (0, 1, 2))
        rs_second(t, 0)
        begin(t, 1)
        store_emitted(t, 0)
        finish(t, 0)
        emission(t + 1, 0)
        rs_merge(t, 1)
        emission(t + 1, 1)
        emission(t + 1, 2)
        if t < STEPS:
            ag_relay(t, 0, (0, 1, 2))
        rs_second(t, 1)
        store_emitted(t, 1)
    finish(STEPS, 1)

    wide = iota((SEQS, 128), 0) == iota((SEQS, 128), 1)
    total = jnp.sum(wfin[:, :BLOCK] + wfin[:, BLOCK:], axis=1, keepdims=True)
    mine = jnp.sum(jnp.where(wide, total, 0.0), axis=0, keepdims=True)
    ar0[0] = jnp.broadcast_to(mine, (8, 128))
    ar1[row] = ar0[0]

    def a1(i):
        return remote(ar0.at[0], ar1.at[row], a_send.at[0], a_recv.at[0], row_peers[i - 1])

    def a2(i):
        return remote(ar0.at[1], ar2.at[col], a_send.at[1], a_recv.at[1], col_peers[i - 1])

    seven = remote(ar1.at[0:7], ar1.at[0:7], a_send.at[0], a_recv.at[0], sib)
    fifteen = remote(ar2.at[0:15], ar2.at[0:15], a_send.at[1], a_recv.at[1], sib)
    for i in range(1, 8):
        a1(i).start()
    seven.wait_recv()
    ar0[1] = jnp.sum(ar1[...], axis=0)
    ar2[col] = ar0[1]
    for i in range(1, 16):
        a2(i).start()
    fifteen.wait_recv()
    scale_ref[...] = jnp.sum(ar2[...], axis=0) * (1.0 / STATES)

    for c in (0, 1):
        rs_sent(STEPS, c)
        ag_sent(STEPS - 1, c)
    e_sent2()
    for t in range(STEPS + 1):
        remote(packs[t], packs[t], e_send.at[t], e_recv.at[t, 0, 0], sib).wait_send()
    seven.wait_send()
    fifteen.wait_send()


def normalize(weights_ref, scale_ref, post_ref, log_ref):
    wide = iota((SEQS, 128), 0) == iota((SEQS, 128), 1)
    scale = scale_ref[0:1, :]
    log_ref[...] = jnp.log(scale[:, :SEQS])
    scale_col = jnp.sum(jnp.where(wide, scale, 0.0), axis=1, keepdims=True)
    post_ref[...] = (weights_ref[...] / scale_col).astype(BF16)


def on_device(blocks, source_ids, emission, tokens):
    vocab = emission.shape[0]
    dma = pltpu.SemaphoreType.DMA
    vmem = pltpu.VMEM
    weights, scale = pl.pallas_call(
        kernel,
        out_shape=(jax.ShapeDtypeStruct((SEQS, 2 * BLOCK), F32), jax.ShapeDtypeStruct((8, 128), F32)),
        in_specs=[
            pl.BlockSpec(memory_space=pltpu.SMEM),
            pl.BlockSpec(memory_space=pltpu.VMEM),
            pl.BlockSpec(memory_space=pl.ANY),
            pl.BlockSpec(memory_space=pl.ANY),
        ],
        out_specs=(pl.BlockSpec(memory_space=pltpu.VMEM), pl.BlockSpec(memory_space=pltpu.VMEM)),
        scratch_shapes=[
            vmem((32, BLOCK, BLOCK), BF16),
            vmem((32, vocab, BLOCK), BF16),
            vmem((SLOT + TIGHT, vocab), BF16),
            vmem((STEPS, 2, 3, 4, SLOT, BLOCK), BF16),
            vmem((2, 3, 4, TIGHT - 2 * SLOT, BLOCK), BF16),
            vmem((STEPS, 2, 4, 4, SLOT, BLOCK), BF16),
            vmem((2, 4, 4, TIGHT - 2 * SLOT, BLOCK), BF16),
            vmem((STEPS + 1, 2, 3, 48, BLOCK), BF16),
            vmem((STEPS + 1, 2, 3, 56, BLOCK), BF16),
            vmem((2, 3, 48, BLOCK), BF16),
            vmem((2, 3, 56, BLOCK), BF16),
            vmem((2, SEQS, BLOCK), BF16),
            vmem((STEPS, 2, SEQS, BLOCK), BF16),
            vmem((16, 48, BLOCK), BF16),
            vmem((16, 48, BLOCK), BF16),
            vmem((16, 56, BLOCK), BF16),
            vmem((16, 56, BLOCK), BF16),
            vmem((2, 4, 4, 48, BLOCK), BF16),
            vmem((2, 4, 4, 56, BLOCK), BF16),
            vmem((2, 2, 15, 48, BLOCK), BF16),
            vmem((2, 2, 15, 56, BLOCK), BF16),
            vmem((2, 8, 128), F32),
            vmem((8, 8, 128), F32),
            vmem((16, 8, 128), F32),
            dma,
            dma((32,)),
            dma((STEPS + 1,)),
            dma((STEPS + 1, 2, 2)),
            dma((2,)),
            dma((STEPS + 1, 2, 2)),
            dma((2, 2)),
            dma((2, 2, 2, 4)),
            dma((2, 2)),
            dma((2, 2, 2, 9)),
            dma((2,)),
            dma((2,)),
        ],
        compiler_params=pltpu.CompilerParams(
            collective_id=0, has_side_effects=True, vmem_limit_bytes=63 * 2**20
        ),
        name="forward",
    )(source_ids.reshape(-1), tokens, blocks.reshape(32, BLOCK, BLOCK), emission)
    posterior, logs = pl.pallas_call(
        normalize,
        out_shape=(jax.ShapeDtypeStruct((SEQS, 2 * BLOCK), BF16), jax.ShapeDtypeStruct((1, SEQS), F32)),
        in_specs=[pl.BlockSpec(memory_space=pltpu.VMEM)] * 2,
        out_specs=(pl.BlockSpec(memory_space=pltpu.VMEM), pl.BlockSpec(memory_space=pltpu.VMEM)),
        name="normalize",
    )(weights, scale)
    return posterior, logs.reshape(SEQS)


def solution(mesh):
    in_specs = (P("row", "col", None, None), P("row", "col"), P("col", "row"), P())
    out_specs = (P(None, ("row", "col")), P())
    return jax.shard_map(on_device, mesh=mesh, in_specs=in_specs, out_specs=out_specs, check_vma=False)
```
